128 devices in a mesh: occ: 4 (over z), vir: 32 (over x, y, core).
Axes of the slice: x: 4, y: 4, z: 4, core: 2. Of those that a mesh axis runs over, the one named last changes fastest.
Arguments:
- amps: bfloat16 [3072, 16384], P('occ', 'vir'), may hold values from -6 to 6
- cycle_amps: bfloat16 [3072, 8192], P(('occ', 'vir')), may hold values from -6 to 6
- cycle_ints: bfloat16 [8192, 16384], P(None, 'vir'), may hold values from -0.0625 to 0.0625
- ladder_ints: bfloat16 [64, 4, 256, 256], P('vir'), may hold values from -0.1875 to 0.1875
- sources: int32 [64, 4], replicated, may hold values from 0 to 63, as said below
- counts: int32 [64], replicated, may hold values from 1 to 4
- eps_occ: float32 [3072], P('occ'), may hold values from 0.5 to 4
- eps_vir: float32 [16384], P('vir'), may hold values from 0.5 to 4
Outputs:
- residual: bfloat16 [3072, 16384], P('occ', 'vir')
- new_amps: bfloat16 [3072, 16384], P('occ', 'vir')
- residual_norm: float32 [], replicated
The draws below stay inside these ranges and needn't reach their ends.
Inputs may be any that keep to these rules, and one draw needn't show every extreme that they name: `sources`: with owner(s) = s // 2: for each group of 2 consecutive target tiles (those of one owner), all 8 entries of their rows name tiles of different owners.
All inputs are finite; a program needn't handle non-finite values.
Results may differ from the reference program's by a relative error of at most 0.012.
Values may be sent and summed in bfloat16 or wider, within the bound.
A program may use at most 128 MiB of HBM per device.

```python
import math
import jax
import jax.numpy as jnp
from jax import lax

TILE = 256
CYCLE_W = 8192
ALLOWED = 4
VT_DEV = 2
VTILES = 64
VP = 16384
OP = 3072


def draw_sources(key, part):
    key = jax.random.fold_in(key, 11)
    owners = VTILES // VT_DEV
    perm_key, pick_key = jax.random.split(key)
    group_keys = jax.random.split(perm_key, owners)
    chosen = jax.vmap(lambda one_key: jax.random.permutation(one_key, owners)[:VT_DEV * ALLOWED])(group_keys)
    picked = jax.random.randint(pick_key, (owners, VT_DEV * ALLOWED), 0, VT_DEV)
    tiles = chosen * VT_DEV + picked
    return tiles.reshape(VTILES, ALLOWED).astype(jnp.int32)


def draw_counts(key, part):
    key = jax.random.fold_in(key, 12)
    first_key, second_key = jax.random.split(key)
    values = jax.random.randint(first_key, (VTILES,), 1, ALLOWED + 1)
    position = jax.random.randint(second_key, (), 0, VTILES)
    values = values.at[position].set(ALLOWED)
    values = values.at[(position + 1) % VTILES].set(1)
    return values.astype(jnp.int32)


def levels(key, shape, cuts, low, high):
    factor_of = 1.0
    for dim, parts in cuts:
        steps = jax.random.uniform(jax.random.fold_in(jax.random.fold_in(key, 6), dim), (parts,), jnp.float32, low / len(cuts), high / len(cuts))
        factor_of = factor_of * jnp.repeat(jnp.exp(steps), shape[dim] // parts).reshape((-1,) + (1,) * (len(shape) - 1 - dim))
    return factor_of


def normal_values(stream_key, dims, spread, bound, pieces=(), kind=jnp.bfloat16):
    values = jax.random.normal(stream_key, dims, jnp.float32) * spread
    if len(pieces) > 0:
        values = levels(stream_key, dims, pieces, -0.22, 0.18) * values
    return jnp.clip(values, min=-bound, max=bound).astype(kind)


def setup_inputs(seed: int = 0) -> dict:
    key_of = jax.random.split(jax.random.key(seed), 9)
    return {
        "amps": normal_values(key_of[0], (OP, VP), 1.0, 6.0, ((0, 4), (1, 32))),
        "cycle_amps": normal_values(key_of[1], (OP, CYCLE_W), 1.0, 6.0, ((0, 128),)),
        "cycle_ints": normal_values(key_of[2], (CYCLE_W, VP), CYCLE_W ** -0.5, 0.0625, ((1, 32),)),
        "ladder_ints": normal_values(key_of[3], (VTILES, ALLOWED, TILE, TILE), (ALLOWED * TILE) ** -0.5, 0.1875, ((0, 32),)),
        "sources": draw_sources(jax.random.fold_in(key_of[8], 71), 0),
        "counts": draw_counts(jax.random.fold_in(key_of[8], 71), 0),
        "eps_occ": jnp.clip(jnp.exp(math.log(4.0) - 2.0794415 * jax.random.uniform(key_of[6], (OP,), jnp.float32) ** levels(key_of[6], (OP,), ((0, 4),), -0.2, 0.2)), 0.5, 4.0),
        "eps_vir": jnp.clip(jnp.exp(math.log(4.0) - 2.0794415 * jax.random.uniform(key_of[7], (VP,), jnp.float32) ** levels(key_of[7], (VP,), ((0, 32),), -0.2, 0.2)), 0.5, 4.0),
    }


def reference(amps, cycle_amps, cycle_ints, ladder_ints, sources, counts, eps_occ, eps_vir):
    cycle = jnp.dot(cycle_amps, cycle_ints, preferred_element_type=jnp.float32).astype(jnp.bfloat16)
    dressed = (amps.astype(jnp.float32) + cycle.astype(jnp.float32)).astype(jnp.bfloat16)
    rows = dressed.shape[0]

    def one_target(target):
        def add_slot(slot, totals):
            source = sources[target, slot]
            column_block = lax.dynamic_slice_in_dim(dressed, (source * TILE).astype(jnp.int32), TILE, 1)
            weight = lax.dynamic_index_in_dim(lax.dynamic_index_in_dim(ladder_ints, target, 0, False), slot, 0, False)
            term = jnp.dot(column_block, weight, preferred_element_type=jnp.float32)
            return totals + jnp.where(slot < counts[target], term, jnp.zeros_like(term))
        return lax.fori_loop(0, ALLOWED, add_slot, jnp.zeros((rows, TILE), jnp.float32))

    stacked = lax.map(one_target, jnp.arange(VTILES, dtype=jnp.int32))
    ladder = jnp.transpose(stacked, (1, 0, 2)).reshape(rows, VTILES * TILE)
    residual = (ladder + cycle.astype(jnp.float32)).astype(jnp.bfloat16)
    res_wide = residual.astype(jnp.float32)
    denom = eps_occ[:, None] + eps_vir[None, :]
    new_amps = (amps.astype(jnp.float32) - res_wide / denom).astype(jnp.bfloat16)
    residual_norm = jnp.sum(res_wide * res_wide)
    return residual, new_amps, residual_norm
```

```python
import functools

import jax
import jax.numpy as jnp
from jax import lax
from jax.experimental import pallas as pl
from jax.experimental.pallas import tpu as pltpu
from jax.sharding import PartitionSpec as P

MESH = pl.DeviceIdType.MESH
RING = 4
DIST = (1, 3, 2)
CAPS = (6, 8, 16)
ORDER = (0, 1, 3, 2)
F32, BF16 = jnp.float32, jnp.bfloat16


def place():
    vir = lax.axis_index("vir")
    core = vir % 2
    y = (vir // 2) % RING
    x = vir // (2 * RING)
    first = jnp.where(core == 0, x, y)
    second = jnp.where(core == 0, y, x)
    return core, first, second, x, y


def tables(sources, counts, sources_v, counts_v, pack, lad, most, before):
    core, p, q, x, y = place()

    def split(tile):
        tx, ty = tile // 16, (tile // 4) % 4
        return jnp.where(core == 0, tx, ty), jnp.where(core == 0, ty, tx), tile % 4

    def asked(chip, line):
        mask = jnp.int32(0)
        for t in range(4):
            for k in range(4):
                tp, tq, tt = split(sources[chip * 4 + t, k])
                hit = (tq == line) & (k < counts[chip * 4 + t])
                mask = mask | jnp.where(hit, jnp.int32(1) << (tp * 4 + tt), 0)
        return mask

    def chip_at(fp, fq):
        return jnp.where(core == 0, fp * 4 + fq, fq * 4 + fp)

    for g, d in enumerate(DIST):
        other = (q + d) % RING
        mask = asked(chip_at(p, other), q)
        for e in range(16):
            pack[g, e] = 0
        n = jnp.int32(0)
        for e in range(16):
            pack[g, n] = e
            n = n + ((mask >> e) & 1)
        mask = asked(chip_at(p, q), other)
        n = jnp.int32(0)
        for e in range(16):
            before[g, e] = n
            n = n + ((mask >> e) & 1)
    mine = x * 4 + y
    for t in range(4):
        for k in range(4):
            tp, tq, tt = split(sources[mine * 4 + t, k])
            live = k < counts[mine * 4 + t]
            local = tq == q
            d = (tq - q + RING) % RING
            g = jnp.where(d == 1, 0, jnp.where(d == 3, 1, 2))
            e = tp * 4 + tt
            slot = t * 4 + k
            lad[0, slot] = jnp.where(live & local, e, p * 4)
            lad[1, slot] = jnp.where(live & ~local, g, 0)
            lad[2, slot] = jnp.where(live & ~local, before[g, e], 0)
            lad[3, slot] = jnp.where(live & ~local, 0, 1)
            lad[4, slot] = jnp.where(live, 1, 0)

    tiles = lax.broadcasted_iota(jnp.int32, (64, 128), 1)
    hits = jnp.zeros((64, 128), F32)
    for k in range(4):
        hits += jnp.where((sources_v[:, k : k + 1] == tiles) & (counts_v[...] > k), 1.0, 0.0)
    group = lax.broadcasted_iota(jnp.int32, (16, 64), 0)
    member = lax.broadcasted_iota(jnp.int32, (16, 64), 1) // 4
    need = jnp.dot(jnp.where(group == member, 1.0, 0.0).astype(BF16), hits.astype(BF16), preferred_element_type=F32)
    need = jnp.minimum(need, 1.0)
    tile = lax.broadcasted_iota(jnp.int32, (128, 128), 0)
    line = lax.broadcasted_iota(jnp.int32, (128, 128), 1)
    inside = ((line < 4) & ((tile // 4) % 4 == line)) | ((line >= 4) & (line < 8) & (tile // 16 == line - 4))
    sums = jnp.dot(need.astype(BF16), jnp.where(inside, 1.0, 0.0).astype(BF16), preferred_element_type=F32)
    chip = lax.broadcasted_iota(jnp.int32, (16, 128), 0)
    line = lax.broadcasted_iota(jnp.int32, (16, 128), 1)
    own = (line == chip % 4) | (line == chip // 4 + 4)
    most[0] = jnp.max(jnp.where(own, 0.0, sums)).astype(jnp.int32)


def make_tables(sources, counts):
    smem, vmem = pl.BlockSpec(memory_space=pltpu.SMEM), pl.BlockSpec(memory_space=pltpu.VMEM)
    return pl.pallas_call(
        tables,
        out_shape=(
            jax.ShapeDtypeStruct((3, 16), jnp.int32),
            jax.ShapeDtypeStruct((5, 16), jnp.int32),
            jax.ShapeDtypeStruct((1,), jnp.int32),
        ),
        in_specs=[smem, smem, vmem, vmem],
        out_specs=(smem, smem, smem),
        scratch_shapes=[pltpu.SMEM((3, 16), jnp.int32)],
    )(sources, counts, sources, counts.reshape(-1, 1))


def main(
    cap, width, pack_i, lad_i, a_ref, b_ref, amp_ref, l_ref, eo_ref, ev_ref,
    res_ref, new_ref, norm_ref,
    abuf, bbuf, ampbuf, lbuf, evbuf, cyc, row0, row1, row2, row3, packs, got0, got1, got2, got3,
    resbuf, newbuf, nacc, nbuf, ssem, rsem, lsem,
):
    core, p, q, x, y = place()
    z = lax.axis_index("occ")
    sister = 1 - core
    rows, got = (row0, row1, row2, row3), (got0, got1, got2, got3)
    half_k = width // 2
    relay = 3 * half_k // 2

    def at(fp, fq):
        fp, fq = fp % RING, fq % RING
        return (z, jnp.where(core == 0, (fp * 4 + fq) * 2, (fq * 4 + fp) * 2 + 1))

    def chip_core(zz, cc):
        return (zz, (x * 4 + y) * 2 + cc)

    partners = [at(p + d, q) for d in DIST] + [at(p, q + d) for d in DIST]
    group = [((z + dz) % 4, (core + dc) % 2) for dz in range(4) for dc in range(2) if dz or dc]
    partners += [chip_core(*one) for one in group]
    barrier = pltpu.get_barrier_semaphore()
    for one in partners:
        pl.semaphore_signal(barrier, inc=1, device_id=one, device_id_type=MESH)

    numbers, made = {}, {}

    def describe(key, src, dst, dev):
        n = numbers.setdefault(key, len(numbers))
        return pltpu.make_async_remote_copy(
            src_ref=src, dst_ref=dst, send_sem=ssem.at[n], recv_sem=rsem.at[n], device_id=dev, device_id_type=MESH
        )

    def send(key, src, dst, dev):
        made[key] = describe(key, src, dst, dev)
        made[key].start()

    def arrived(key):
        made[key].wait_recv()

    loads = []

    def load(src, dst):
        one = pltpu.make_async_copy(src, dst, lsem.at[len(loads)])
        one.start()
        loads.append(one)
        return one

    own_b = load(b_ref, bbuf.at[core])
    own_amp = load(amp_ref.at[core], ampbuf.at[core])
    own_l = load(l_ref, lbuf.at[core])

    for at_col in range(0, half_k, 1024):
        left = a_ref[:, at_col : at_col + 1024].astype(F32)
        right = a_ref[:, half_k + at_col : half_k + at_col + 1024].astype(F32)
        abuf[0, p, :, at_col : at_col + 1024] = left[:16].astype(BF16)
        abuf[0, p, :, half_k + at_col : half_k + at_col + 1024] = right[:16].astype(BF16)
        abuf[0, p, :, width + at_col : width + at_col + 1024] = jnp.concatenate([left[16:], right[16:]], axis=0).astype(BF16)
    evbuf[core] = ev_ref[...]

    pl.semaphore_wait(barrier, len(partners))

    firsthalf, secondhalf = pl.ds(0, relay), pl.ds(relay, relay)

    def along_first(i):
        if i == 3:
            pp = (p + 3) % RING
            send(("a1r", 3), abuf.at[0, pp, :, firsthalf], abuf.at[0, pp, :, firsthalf], at(p + 1, q))
        else:
            pp = (p + 1) % RING
            send(("a1r", 1), abuf.at[0, pp, :, secondhalf], abuf.at[0, pp, :, secondhalf], at(p - 1, q))

    def spread(i):
        pp = (p + i) % RING
        send(("a2", i, 1), abuf.at[0, pp], abuf.at[3, pp], at(p, q + 1))
        send(("a2", i, 3), abuf.at[0, pp], abuf.at[1, pp], at(p, q - 1))

    def pass_on(i):
        pp = (p + i) % RING
        arrived(("a2", i, 1))
        send(("a2r", i, 1), abuf.at[3, pp, :, firsthalf], abuf.at[2, pp, :, firsthalf], at(p, q + 1))
        arrived(("a2", i, 3))
        send(("a2r", i, 3), abuf.at[1, pp, :, secondhalf], abuf.at[2, pp, :, secondhalf], at(p, q - 1))

    send(("a1", 1), abuf.at[0, p], abuf.at[0, p], at(p + 1, q))
    send(("a1", 3), abuf.at[0, p], abuf.at[0, p], at(p - 1, q))
    spread(0)
    to_sister = chip_core(z, sister)
    send("b", b_ref, bbuf.at[core], to_sister)
    send("amp", amp_ref.at[sister], ampbuf.at[core], to_sister)
    send("l", l_ref, lbuf.at[core], to_sister)
    send("ev", ev_ref, evbuf.at[core], to_sister)

    arrived(("a1", 1))
    along_first(3)
    arrived(("a1", 3))
    along_first(1)
    spread(3)
    spread(1)
    pass_on(0)
    arrived(("a1r", 3))
    arrived(("a1r", 1))
    spread(2)

    def multiply(j):
        row = (q + j) % RING

        def one_tile(t, carry):
            cc = t // 2
            cols = pl.ds(pl.multiple_of((t % 2) * 256, 256), 256)
            low = abuf[j, :, :, 0:half_k].reshape(64, half_k)
            high = abuf[j, :, :, half_k:width].reshape(64, half_k)
            tail = abuf[j, :, :, width : width + half_k].reshape(64, half_k)
            sum0 = jnp.dot(
                jnp.concatenate([low, tail], axis=0), bbuf[cc, 0:half_k, cols], preferred_element_type=F32
            )
            sum1 = jnp.dot(
                jnp.concatenate([high, tail], axis=0), bbuf[cc, half_k:width, cols], preferred_element_type=F32
            )
            main_rows = sum0[:64] + sum1[:64]
            tail_rows = sum0[64:].reshape(4, 2, 8, 256)[:, 0] + sum1[64:].reshape(4, 2, 8, 256)[:, 1]
            cycle = jnp.concatenate([main_rows, tail_rows.reshape(32, 256)], axis=0).astype(BF16)
            cyc[j, t] = cycle
            amps = ampbuf[cc, row, :, cols].astype(F32)
            rows[j][p * 4 + t] = (amps + cycle.astype(F32)).astype(BF16)
            return carry

        lax.fori_loop(0, 4, one_tile, 0)

    def share(j):
        mine = pl.ds(p * 4, 4)
        send(("e1", j, 1), rows[j].at[mine], rows[j].at[mine], at(p + 1, q))
        send(("e1", j, 3), rows[j].at[mine], rows[j].at[mine], at(p - 1, q))

    def share_on(j):
        arrived(("e1", j, 1))
        two = pl.ds(((p + 3) % RING) * 4, 2)
        send(("e1r", j, 1), rows[j].at[two], rows[j].at[two], at(p + 1, q))
        arrived(("e1", j, 3))
        two = pl.ds(((p + 1) % RING) * 4 + 2, 2)
        send(("e1r", j, 3), rows[j].at[two], rows[j].at[two], at(p - 1, q))

    def hand_out(j):
        arrived(("e1r", j, 1))
        arrived(("e1r", j, 3))
        for g, d in enumerate(DIST):

            def one_slot(s, carry, g=g):
                packs[j, g * cap + s] = rows[j][pack_i[g, s]]
                return carry

            lax.fori_loop(0, cap, one_slot, 0)
            there = DIST.index((-d) % RING)
            send(
                ("e2", j, g), packs.at[j, pl.ds(g * cap, cap)], got[(j - d) % RING].at[pl.ds(there * cap, cap)],
                at(p, q + d),
            )

    own_b.wait()
    own_amp.wait()
    own_l.wait()
    arrived("amp")
    arrived("ev")
    arrived("l")

    def mask_weights(s, carry):
        t, k = s // 4, s % 4
        slot = (t % 2) * 4 + k
        lbuf[t // 2, slot] = lbuf[t // 2, slot] * lad_i[4, s].astype(F32).astype(BF16)
        return carry

    lax.fori_loop(0, 16, mask_weights, 0)
    pass_on(3)
    pass_on(1)
    arrived("b")
    multiply(0)
    share(0)
    pass_on(2)
    share_on(0)
    multiply(1)
    share(1)
    multiply(3)
    share(3)
    hand_out(0)
    share_on(1)
    share_on(3)
    for i in range(RING):
        arrived(("a2r", i, 1))
        arrived(("a2r", i, 3))
    multiply(2)
    share(2)
    hand_out(1)
    share_on(2)
    hand_out(3)
    hand_out(2)

    nacc[...] = jnp.zeros_like(nacc)

    def finish(j):
        for g, d in enumerate(DIST):
            arrived(("e2", (j - d) % RING, DIST.index((-d) % RING)))
        row = (q + j) % RING

        def one_tile(t, carry):
            cc = t // 2
            cols = pl.ds(pl.multiple_of((t % 2) * 256, 256), 256)
            total = jnp.zeros((96, 256), F32)
            for k in range(4):
                s = t * 4 + k
                near = rows[j][lad_i[0, s]].astype(F32)
                far = got[j][lad_i[1, s] * cap + lad_i[2, s]].astype(F32)
                block = jnp.where(lad_i[3, s] == 1, near, far).astype(BF16)
                total += jnp.dot(block, lbuf[cc, (t % 2) * 4 + k], preferred_element_type=F32)
            residual = (total + cyc[j, t].astype(F32)).astype(BF16)
            wide = residual.astype(F32)
            denom = eo_ref[row] + evbuf[cc, 0:1, cols]
            resbuf[j, cc, :, cols] = residual
            newbuf[j, cc, :, cols] = (ampbuf[cc, row, :, cols].astype(F32) - wide / denom).astype(BF16)
            nacc[...] += (wide * wide).reshape(12, 8, 256).sum(axis=0)
            return carry

        lax.fori_loop(0, 4, one_tile, 0)
        load(resbuf.at[j, core], res_ref.at[core, row])
        load(newbuf.at[j, core], new_ref.at[core, row])
        send(("res", j), resbuf.at[j, sister], res_ref.at[core, row], to_sister)
        send(("new", j), newbuf.at[j, sister], new_ref.at[core, row], to_sister)

    for j in (2, 0, 1, 3):
        finish(j)

    value = jnp.sum(nacc[...])
    line = ([(q + d) % 4 for d in DIST], q, [at(p, q + d) for d in DIST])
    ring = ([(p + d) % 4 for d in DIST], p, [at(p + d, q) for d in DIST])
    rest = (None, z * 2 + core, [chip_core(*one) for one in group])
    for stage, (_, slot, devices) in enumerate((line, ring, rest)):
        nbuf[stage, slot] = jnp.full((8, 128), value, F32)
        for n, dev in enumerate(devices):
            send(("n", stage, n), nbuf.at[stage, slot], nbuf.at[stage, slot], dev)
        for n in range(len(devices)):
            arrived(("n", stage, n))
        total = nbuf[stage, 0]
        for n in range(1, len(devices) + 1):
            total = total + nbuf[stage, n]
        if stage < 2:
            value = total
            value = jnp.max(value)
    norm_ref[...] = total

    for j in range(RING):
        arrived(("res", j))
        arrived(("new", j))
    for one in loads[3:]:
        one.wait()
    for one in made.values():
        one.wait_send()


COPIES = 80


def run_main(cap, number, pack, lad, a, b, amp, blocks, eo, ev):
    width, columns = b.shape
    rows = amp.shape[2]
    smem, vmem = pl.BlockSpec(memory_space=pltpu.SMEM), pl.BlockSpec(memory_space=pltpu.VMEM)
    anywhere = pl.BlockSpec(memory_space=pl.ANY)
    out = jax.ShapeDtypeStruct((2, RING, rows, columns), BF16)
    row_buf = pltpu.VMEM((16, rows, 256), BF16)
    got_buf = pltpu.VMEM((3 * cap, rows, 256), BF16)
    return pl.pallas_call(
        functools.partial(main, cap, width),
        out_shape=(out, out, jax.ShapeDtypeStruct((8, 128), F32)),
        in_specs=[smem, smem, vmem, anywhere, anywhere, anywhere, vmem, vmem],
        out_specs=(anywhere, anywhere, vmem),
        scratch_shapes=[
            pltpu.VMEM((RING, RING, 16, width + width // 2), BF16),
            pltpu.VMEM((2, width, columns), BF16),
            pltpu.VMEM((2, RING, rows, columns), BF16),
            pltpu.VMEM((2, 8, 256, 256), BF16),
            pltpu.VMEM((2, 8, columns), F32),
            pltpu.VMEM((RING, 4, rows, 256), BF16),
            row_buf, row_buf, row_buf, row_buf,
            pltpu.VMEM((RING, 3 * cap, rows, 256), BF16),
            got_buf, got_buf, got_buf, got_buf,
            pltpu.VMEM((RING, 2, rows, columns), BF16),
            pltpu.VMEM((RING, 2, rows, columns), BF16),
            pltpu.VMEM((8, 256), F32),
            pltpu.VMEM((3, 8, 8, 128), F32),
            pltpu.SemaphoreType.DMA((COPIES,)),
            pltpu.SemaphoreType.DMA((COPIES,)),
            pltpu.SemaphoreType.DMA((11,)),
        ],
        compiler_params=pltpu.CompilerParams(
            collective_id=number, has_side_effects=True, vmem_limit_bytes=60 * 2**20
        ),
        cost_estimate=pl.CostEstimate(flops=8 * 10**9, bytes_accessed=20 * 2**20, transcendentals=0),
    )(pack, lad, a, b, amp, blocks, eo, ev)


def to_core_rows(array):
    rest = array.shape[1:]
    blocks = array.reshape(RING, RING, 2, 24, *rest)
    swap = (1, 0) + tuple(range(2, 3 + len(rest)))
    both = jnp.stack([blocks[:, :, 0].transpose(swap), blocks[:, :, 1]])
    return jnp.concatenate(
        [both[:, :, :, :16].reshape(2, RING, 64, *rest), both[:, :, :, 16:].reshape(2, RING, 32, *rest)], axis=2
    )


def from_core_rows(array):
    rest = array.shape[3:]
    both = jnp.concatenate(
        [array[:, :, :64].reshape(2, RING, RING, 16, *rest), array[:, :, 64:].reshape(2, RING, RING, 8, *rest)], axis=3
    )
    swap = (1, 0) + tuple(range(2, 3 + len(rest)))
    return jnp.stack([both[0].transpose(swap), both[1]], axis=2).reshape(RING * RING * 2 * 24, *rest)


def on_device(amps, cycle_amps, cycle_ints, ladder_ints, sources, counts, eps_occ, eps_vir):
    core = lax.axis_index("vir") % 2
    pack, lad, most = make_tables(sources, counts)
    amp = to_core_rows(amps)
    eo = lax.dynamic_index_in_dim(to_core_rows(eps_occ), core, 0, False)[..., None]
    ev = jnp.broadcast_to(eps_vir[None, :], (8, eps_vir.shape[0]))
    blocks = ladder_ints.reshape(8, *ladder_ints.shape[2:])
    branches = [functools.partial(run_main, cap, n) for n, cap in enumerate(CAPS)]
    which = sum((most[0] > cap).astype(jnp.int32) for cap in CAPS[:-1])
    residual, new_amps, norm = lax.switch(
        which, branches, pack, lad, cycle_amps, cycle_ints, amp, blocks, eo, ev
    )
    return from_core_rows(residual), from_core_rows(new_amps), norm[0, 0]


def solution(mesh):
    placed = (
        P("occ", "vir"),
        P(("occ", "vir"), None),
        P(None, "vir"),
        P("vir", None, None, None),
        P(),
        P(),
        P("occ"),
        P("vir"),
    )
    return jax.shard_map(
        on_device,
        mesh=mesh,
        in_specs=placed,
        out_specs=(P("occ", "vir"), P("occ", "vir"), P()),
        check_vma=False,
    )
```

```python
import functools

import jax
import jax.numpy as jnp
from jax import lax
from jax.experimental import pallas as pl
from jax.experimental.pallas import tpu as pltpu
from jax.sharding import PartitionSpec as P

MESH = pl.DeviceIdType.MESH
RING = 4
DIST = (1, 3, 2)
CAPS = (6, 8, 16)
ORDER = (0, 1, 3, 2)
F32, BF16 = jnp.float32, jnp.bfloat16


def place():
    vir = lax.axis_index("vir")
    core = vir % 2
    y = (vir // 2) % RING
    x = vir // (2 * RING)
    first = jnp.where(core == 0, x, y)
    second = jnp.where(core == 0, y, x)
    return core, first, second, x, y


def tables(sources, counts, plan, which):
    core, p, q, x, y = place()

    def iota(shape, axis):
        return lax.broadcasted_iota(jnp.int32, shape, axis)

    def ones(mask):
        return jnp.where(mask, 1.0, 0.0)

    def dot(one, other):
        return jnp.dot(one.astype(BF16), other.astype(BF16), preferred_element_type=F32)

    def split(tile):
        tx, ty = tile // 16, (tile // 4) % 4
        return jnp.where(core == 0, tx, ty), jnp.where(core == 0, ty, tx), tile % 4

    tile = iota((64, 64), 0)
    hits = jnp.zeros((64, 64), F32)
    for k in range(4):
        hits += ones((sources[k : k + 1, :] == tile) & (counts[...] > k))
    need = jnp.minimum(dot(hits, ones(iota((64, 128), 0) // 4 == iota((64, 128), 1))), 1.0)

    line, member = iota((16, 64), 0), iota((16, 64), 1)
    inside = ((line < 4) & ((member // 4) % 4 == line)) | ((line >= 4) & (line < 8) & (member // 16 == line - 4))
    line, chip = iota((16, 128), 0), iota((16, 128), 1)
    own = ((line < 4) & (chip % 4 == line)) | (chip // 4 + 4 == line)
    most = jnp.max(jnp.where(own, 0.0, dot(ones(inside), need))).astype(jnp.int32)
    branch, cap = jnp.int32(0), jnp.int32(CAPS[0])
    for n, limit in enumerate(CAPS[:-1]):
        branch = jnp.where(most > limit, n + 1, branch)
        cap = jnp.where(most > limit, CAPS[n + 1], cap)
    which[0] = branch

    tp, tq, tt = split(tile)
    op, oq, ot = split(iota((64, 64), 1))
    placed = dot(ones((tq == oq) & (op * 4 + ot < tp * 4 + tt)), need)
    sp, sq, st = split(iota((64, 1), 0))
    entry = (sp * 4 + st).astype(F32)
    chip, slot = iota((64, 128), 1), iota((64, 128), 1).astype(F32)
    plan[...] = jnp.zeros_like(plan)
    for g, d in enumerate(DIST):
        other = (q + d) % RING
        there = chip == jnp.where(core == 0, p * 4 + other, other * 4 + p)
        wants = jnp.sum(jnp.where(there, need, 0.0), axis=1, keepdims=True)
        where = jnp.sum(jnp.where(there, placed, 0.0), axis=1, keepdims=True)
        taken = (wants > 0.0) & (sq == q) & (where == slot)
        plan[g : g + 1, :] = jnp.sum(jnp.where(taken, entry, 0.0), axis=0, keepdims=True).astype(jnp.int32)
    where = jnp.sum(jnp.where(chip == x * 4 + y, placed, 0.0), axis=1, keepdims=True)
    for k in range(4):
        source = sources[k : k + 1, :]
        tp, tq, tt = split(source)
        after = jnp.sum(jnp.where(source == tile, where, 0.0), axis=0, keepdims=True).astype(jnp.int32)
        live = counts[...] > k
        near = tq == q
        d = (tq - q + RING) % RING
        group = jnp.where(d == 1, 0, jnp.where(d == 3, 1, 2))
        plan[4 + k : 5 + k, 0:64] = jnp.where(live & near, tp * 4 + tt, p * 4)
        plan[8 + k : 9 + k, 0:64] = jnp.where(live & ~near, group * cap + after, 0)
        plan[12 + k : 13 + k, 0:64] = jnp.where(live & ~near, 0, 1)
        plan[16 + k : 17 + k, 0:64] = jnp.where(live, 1, 0)


def make_tables(sources, counts):
    smem, vmem = pl.BlockSpec(memory_space=pltpu.SMEM), pl.BlockSpec(memory_space=pltpu.VMEM)
    return pl.pallas_call(
        tables,
        out_shape=(jax.ShapeDtypeStruct((24, 128), jnp.int32), jax.ShapeDtypeStruct((1,), jnp.int32)),
        in_specs=[vmem, vmem],
        out_specs=(vmem, smem),
    )(sources.T, counts.reshape(1, -1))


def main(
    cap, width, plan, a_ref, b_ref, amp_ref, l_ref, eo_ref, ev_ref,
    res_ref, new_ref, norm_ref,
    abuf, bbuf, amps_mine, amps_away, ampbuf, lbuf, occ, cyc, row0, row1, row2, row3, packs, got0, got1, got2, got3,
    resbuf, resin, nacc, nbuf, ssem, rsem, lsem,
):
    core, p, q, x, y = place()
    z = lax.axis_index("occ")
    sister = 1 - core
    rows, got = (row0, row1, row2, row3), (got0, got1, got2, got3)
    half_k = width // 2
    relay = 3 * half_k // 2

    def at(fp, fq):
        fp, fq = fp % RING, fq % RING
        return (z, jnp.where(core == 0, (fp * 4 + fq) * 2, (fq * 4 + fp) * 2 + 1))

    def on_chip(zz, cc):
        return (zz, (x * 4 + y) * 2 + cc)

    group = [on_chip((z + dz) % 4, (core + dc) % 2) for dz in (2, 1, 3, 0) for dc in (1, 0) if dz or dc]
    plane = [at(p + dp, q + dq) for dp in (2, 1, 3, 0) for dq in (2, 1, 3, 0) if dp or dq]
    partners = group + plane
    barrier = pltpu.get_barrier_semaphore()
    for one in partners:
        pl.semaphore_signal(barrier, inc=1, device_id=one, device_id_type=MESH)

    made = {}

    def send(key, src, dst, dev):
        n = len(made)
        made[key] = pltpu.make_async_remote_copy(
            src_ref=src, dst_ref=dst, send_sem=ssem.at[n], recv_sem=rsem.at[n], device_id=dev, device_id_type=MESH
        )
        made[key].start()

    def arrived(key):
        made[key].wait_recv()

    own_b = pltpu.make_async_copy(b_ref, bbuf.at[core], lsem.at[0])
    own_l = pltpu.make_async_copy(l_ref, lbuf.at[core], lsem.at[1])
    own_b.start()
    own_l.start()

    for at_col in range(0, half_k, 1024):
        left = a_ref[:, at_col : at_col + 1024].astype(F32)
        right = a_ref[:, half_k + at_col : half_k + at_col + 1024].astype(F32)
        abuf[0, p, :, at_col : at_col + 1024] = left[:16].astype(BF16)
        abuf[0, p, :, half_k + at_col : half_k + at_col + 1024] = right[:16].astype(BF16)
        abuf[0, p, :, width + at_col : width + at_col + 1024] = jnp.concatenate([left[16:], right[16:]], axis=0).astype(BF16)

    pl.semaphore_wait(barrier, len(partners))

    halves = (pl.ds(0, relay), pl.ds(relay, relay))

    def along_first(way, h):
        send(("a1", way, h), abuf.at[0, p, :, halves[h]], abuf.at[0, p, :, halves[h]], at(p + way, q))

    def spread(i):
        pp = (p + i) % RING
        for n in range(2):
            send(("a2", i, 1, n), abuf.at[0, pp, :, halves[n]], abuf.at[3, pp, :, halves[n]], at(p, q + 1))
            m = 1 - n
            send(("a2", i, -1, m), abuf.at[0, pp, :, halves[m]], abuf.at[1, pp, :, halves[m]], at(p, q - 1))

    def pass_on(i):
        pp = (p + i) % RING
        arrived(("a2", i, 1, 0))
        send(("a2r", i, 1), abuf.at[3, pp, :, halves[0]], abuf.at[2, pp, :, halves[0]], at(p, q + 1))
        arrived(("a2", i, -1, 1))
        send(("a2r", i, -1), abuf.at[1, pp, :, halves[1]], abuf.at[2, pp, :, halves[1]], at(p, q - 1))

    along_first(1, 0)
    along_first(-1, 1)
    along_first(1, 1)
    along_first(-1, 0)
    to_sister = on_chip(z, sister)
    send("b", b_ref, bbuf.at[core], to_sister)
    send("l", l_ref, lbuf.at[core], to_sister)

    def amps_of(cc, keep):
        for fq in range(RING):
            for pair in range(0, RING, 2):
                tails = []
                for fp in (pair, pair + 1):
                    chip = fp * 4 + fq if cc == 0 else fq * 4 + fp
                    block = amp_ref[48 * chip : 48 * chip + 48, :].astype(F32)
                    block = block[24 * cc : 24 * cc + 24]
                    keep[fq, 16 * fp : 16 * fp + 16, :] = block[:16].astype(BF16)
                    tails.append(block[16:])
                keep[fq, 64 + 8 * pair : 80 + 8 * pair, :] = jnp.concatenate(tails, axis=0).astype(BF16)

    @pl.when(core == 0)
    def _():
        amps_of(0, amps_mine)
        amps_of(1, amps_away)

    @pl.when(core == 1)
    def _():
        amps_of(1, amps_mine)
        amps_of(0, amps_away)

    send("amp", amps_away, ampbuf, to_sister)

    pp, pm = (p + 1) % RING, (p + 3) % RING
    arrived(("a1", 1, 0))
    send(("a1r", 1), abuf.at[0, pm, :, halves[0]], abuf.at[0, pm, :, halves[0]], at(p + 1, q))
    arrived(("a1", -1, 1))
    send(("a1r", -1), abuf.at[0, pp, :, halves[1]], abuf.at[0, pp, :, halves[1]], at(p - 1, q))
    spread(0)
    for part in range(eo_ref.shape[1] // 128):
        values = jnp.broadcast_to(eo_ref[:, part * 128 : part * 128 + 128], (128, 128))
        occ[part * 128 : part * 128 + 128, :] = values.T
    arrived(("a1", 1, 1))
    spread(3)
    arrived(("a1", -1, 0))
    spread(1)
    arrived(("a1r", 1))
    arrived(("a1r", -1))
    spread(2)

    def multiply(j, first, tiles):
        row = (q + j) % RING

        def one_tile(n, carry):
            cc = (core + n // 2) % 2
            t = cc * 2 + n % 2
            cols = pl.ds(pl.multiple_of((t % 2) * 256, 256), 256)
            low = abuf[j, :, :, 0:half_k].reshape(64, half_k)
            high = abuf[j, :, :, half_k:width].reshape(64, half_k)
            tail = abuf[j, :, :, width : width + half_k].reshape(64, half_k)
            sum0 = jnp.dot(
                jnp.concatenate([low, tail], axis=0), bbuf[cc, 0:half_k, cols], preferred_element_type=F32
            )
            sum1 = jnp.dot(
                jnp.concatenate([high, tail], axis=0), bbuf[cc, half_k:width, cols], preferred_element_type=F32
            )
            main_rows = sum0[:64] + sum1[:64]
            tail_rows = sum0[64:].reshape(4, 2, 8, 256)[:, 0] + sum1[64:].reshape(4, 2, 8, 256)[:, 1]
            cycle = jnp.concatenate([main_rows, tail_rows.reshape(32, 256)], axis=0).astype(BF16)
            cyc[j, t] = cycle
            amps = jnp.where(cc == core, amps_mine[row, :, cols].astype(F32), ampbuf[row, :, cols].astype(F32))
            rows[j][p * 4 + t] = (amps + cycle.astype(F32)).astype(BF16)
            return carry

        lax.fori_loop(first, first + tiles, one_tile, 0)

    def share(j):
        mine = pl.ds(p * 4, 4)
        send(("e1", j, 1), rows[j].at[mine], rows[j].at[mine], at(p + 1, q))
        send(("e1", j, -1), rows[j].at[mine], rows[j].at[mine], at(p - 1, q))

    def share_on(j):
        arrived(("e1", j, 1))
        two = pl.ds(pm * 4, 2)
        send(("e1r", j, 1), rows[j].at[two], rows[j].at[two], at(p + 1, q))
        arrived(("e1", j, -1))
        two = pl.ds(pp * 4 + 2, 2)
        send(("e1r", j, -1), rows[j].at[two], rows[j].at[two], at(p - 1, q))

    def hand_out(j):
        arrived(("e1r", j, 1))
        arrived(("e1r", j, -1))
        for g in (2, 0, 1):
            d = DIST[g]

            def one_slot(s, carry, g=g):
                packs[j, g * cap + s] = rows[j][plan[g, s]]
                return carry

            lax.fori_loop(0, cap, one_slot, 0)
            there = DIST.index((-d) % RING)
            send(
                ("e2", j, g), packs.at[j, pl.ds(g * cap, cap)], got[(j - d) % RING].at[pl.ds(there * cap, cap)],
                at(p, q + d),
            )

    pass_on(0)
    own_b.wait()
    arrived("amp")
    multiply(0, 0, 2)
    pass_on(3)
    arrived("b")
    multiply(0, 2, 2)
    share(0)
    pass_on(1)
    own_l.wait()
    arrived("l")
    mine = (x * 4 + y) * 4

    def mask_weights(s, carry):
        t, k = s // 4, s % 4
        slot = (t % 2) * 4 + k
        lbuf[t // 2, slot] = lbuf[t // 2, slot] * plan[16 + k, mine + t].astype(F32).astype(BF16)
        return carry

    lax.fori_loop(0, 16, mask_weights, 0)
    share_on(0)
    pass_on(2)
    for i in range(RING):
        arrived(("a2", i, 1, 1))
    multiply(3, 0, 4)
    share(3)
    for i in range(RING):
        arrived(("a2", i, -1, 0))
    hand_out(0)
    multiply(1, 0, 4)
    share(1)
    share_on(3)
    for i in range(RING):
        arrived(("a2r", i, 1))
        arrived(("a2r", i, -1))
    hand_out(3)
    multiply(2, 0, 4)
    share(2)
    share_on(1)
    hand_out(1)
    share_on(2)
    hand_out(2)

    nacc[...] = jnp.zeros_like(nacc)

    def finish(j):
        for g, d in enumerate(DIST):
            arrived(("e2", (j - d) % RING, DIST.index((-d) % RING)))
        row = (q + j) % RING

        def one_tile(t, carry):
            cols = pl.ds(pl.multiple_of((t % 2) * 256, 256), 256)
            total = jnp.zeros((96, 256), F32)
            for k in range(4):
                near = rows[j][plan[4 + k, mine + t]].astype(F32)
                far = got[j][plan[8 + k, mine + t]].astype(F32)
                block = jnp.where(plan[12 + k, mine + t] == 1, near, far).astype(BF16)
                total += jnp.dot(block, lbuf[t // 2, (t % 2) * 4 + k], preferred_element_type=F32)
            residual = (total + cyc[j, t].astype(F32)).astype(BF16)
            wide = residual.astype(F32)
            resbuf[t // 2, row, :, cols] = residual
            nacc[...] += (wide * wide).reshape(12, 8, 256).sum(axis=0)
            return carry

        lax.fori_loop(0, 4, one_tile, 0)
        send(("res", j), resbuf.at[sister, row], resin.at[row], to_sister)

    for j in (2, 0, 3, 1):
        finish(j)

    def write(first, last):
        def rows_of(cc, fq, fp):
            pair = 64 + 16 * (fp // 2)
            head = jnp.where(core == cc, resbuf[cc, fq, 16 * fp : 16 * fp + 16, :].astype(F32), resin[fq, 16 * fp : 16 * fp + 16, :].astype(F32))
            tail = jnp.where(core == cc, resbuf[cc, fq, pair : pair + 16, :].astype(F32), resin[fq, pair : pair + 16, :].astype(F32))
            return [head, tail[8 * (fp % 2) : 8 * (fp % 2) + 8]]

        for chip in range(first, last):
            fx, fy = chip // 4, chip % 4
            block = jnp.concatenate(rows_of(0, fy, fx) + rows_of(1, fx, fy), axis=0)
            here = slice(48 * chip, 48 * chip + 48)
            lanes = occ[here, :]
            denom = jnp.concatenate([lanes] * (block.shape[1] // 128), axis=1) + ev_ref[...]
            res_ref[here, :] = block.astype(BF16)
            new_ref[here, :] = (amp_ref[here, :].astype(F32) - block / denom).astype(BF16)

    def spread_norm(stage, slot, value, devices):
        nbuf[stage, slot] = jnp.full((8, 128), value, F32)
        for n, dev in enumerate(devices):
            send(("n", stage, n), nbuf.at[stage, slot], nbuf.at[stage, slot], dev)

    def sum_norm(stage, devices):
        for n in range(len(devices)):
            arrived(("n", stage, n))
        total = nbuf[stage, 0]
        for n in range(1, len(devices) + 1):
            total = total + nbuf[stage, n]
        return jnp.max(total)

    spread_norm(0, z * 2 + core, jnp.sum(nacc[...]), group)
    for j in range(RING):
        arrived(("res", j))
    write(0, 8)
    spread_norm(1, p * 4 + q, sum_norm(0, group), plane)
    write(8, 16)
    norm_ref[0] = sum_norm(1, plane)
    for one in made.values():
        one.wait_send()


COPIES = 96


def run_main(cap, number, plan, a, b, amp, blocks, eo, ev):
    width, columns = b.shape
    rows = amp.shape[0] // 8
    smem, vmem = pl.BlockSpec(memory_space=pltpu.SMEM), pl.BlockSpec(memory_space=pltpu.VMEM)
    anywhere = pl.BlockSpec(memory_space=pl.ANY)
    out = jax.ShapeDtypeStruct(amp.shape, BF16)
    row_buf = pltpu.VMEM((16, rows, 256), BF16)
    got_buf = pltpu.VMEM((3 * cap, rows, 256), BF16)
    part = pltpu.VMEM((RING, rows, columns), BF16)
    return pl.pallas_call(
        functools.partial(main, cap, width),
        out_shape=(out, out, jax.ShapeDtypeStruct((1,), F32)),
        in_specs=[smem, vmem, anywhere, vmem, anywhere, vmem, vmem],
        out_specs=(vmem, vmem, smem),
        scratch_shapes=[
            pltpu.VMEM((RING, RING, 16, width + width // 2), BF16),
            pltpu.VMEM((2, width, columns), BF16),
            part, part, part,
            pltpu.VMEM((2, 8, 256, 256), BF16),
            pltpu.VMEM((amp.shape[0], 128), F32),
            pltpu.VMEM((RING, 4, rows, 256), BF16),
            row_buf, row_buf, row_buf, row_buf,
            pltpu.VMEM((RING, 3 * cap, rows, 256), BF16),
            got_buf, got_buf, got_buf, got_buf,
            pltpu.VMEM((2, RING, rows, columns), BF16),
            part,
            pltpu.VMEM((8, 256), F32),
            pltpu.VMEM((2, 16, 8, 128), F32),
            pltpu.SemaphoreType.DMA((COPIES,)),
            pltpu.SemaphoreType.DMA((COPIES,)),
            pltpu.SemaphoreType.DMA((2,)),
        ],
        compiler_params=pltpu.CompilerParams(
            collective_id=number, has_side_effects=True, vmem_limit_bytes=60 * 2**20
        ),
        cost_estimate=pl.CostEstimate(flops=8 * 10**9, bytes_accessed=20 * 2**20, transcendentals=0),
    )(plan, a, b, amp, blocks, eo, ev)


def on_device(amps, cycle_amps, cycle_ints, ladder_ints, sources, counts, eps_occ, eps_vir):
    plan, which = make_tables(sources, counts)
    blocks = ladder_ints.reshape(8, *ladder_ints.shape[2:])
    branches = [functools.partial(run_main, cap, n) for n, cap in enumerate(CAPS)]
    residual, new_amps, norm = lax.switch(
        which[0], branches, plan, cycle_amps, cycle_ints, amps, blocks, eps_occ.reshape(1, -1), eps_vir.reshape(1, -1)
    )
    return residual, new_amps, norm[0]


def solution(mesh):
    placed = (
        P("occ", "vir"),
        P(("occ", "vir"), None),
        P(None, "vir"),
        P("vir", None, None, None),
        P(),
        P(),
        P("occ"),
        P("vir"),
    )
    return jax.shard_map(
        on_device,
        mesh=mesh,
        in_specs=placed,
        out_specs=(P("occ", "vir"), P("occ", "vir"), P()),
        check_vma=False,
    )
```

```python
import functools

import jax
import jax.numpy as jnp
from jax import lax
from jax.experimental import pallas as pl
from jax.experimental.pallas import tpu as pltpu
from jax.sharding import PartitionSpec as P

MESH = pl.DeviceIdType.MESH
RING = 4
DIST = (1, 3, 2)
CAPS = ((6, 5), (6, 6), (8, 8), (16, 16))
PART = 2048
F32, BF16 = jnp.float32, jnp.bfloat16


def place():
    vir = lax.axis_index("vir")
    core = vir % 2
    y = (vir // 2) % RING
    x = vir // (2 * RING)
    first = jnp.where(core == 0, x, y)
    second = jnp.where(core == 0, y, x)
    return core, first, second, x, y


def tables(sources, counts, plan, which):
    core, p, q, x, y = place()

    def iota(shape, axis):
        return lax.broadcasted_iota(jnp.int32, shape, axis)

    def ones(mask):
        return jnp.where(mask, 1.0, 0.0)

    def dot(one, other):
        return jnp.dot(one.astype(BF16), other.astype(BF16), preferred_element_type=F32)

    def split(tile):
        tx, ty = tile // 16, (tile // 4) % 4
        return jnp.where(core == 0, tx, ty), jnp.where(core == 0, ty, tx), tile % 4

    tile = iota((64, 64), 0)
    hits = jnp.zeros((64, 64), F32)
    for k in range(4):
        hits += ones((sources[k : k + 1, :] == tile) & (counts[...] > k))
    need = jnp.minimum(dot(hits, ones(iota((64, 128), 0) // 4 == iota((64, 128), 1))), 1.0)

    line, member = iota((16, 64), 0), iota((16, 64), 1)
    inside = ((line < 4) & ((member // 4) % 4 == line)) | ((line >= 4) & (line < 8) & (member // 16 == line - 4))
    line, chip = iota((16, 128), 0), iota((16, 128), 1)
    sums = dot(ones(inside), need)
    away = jnp.where(line < 4, line - chip % 4, line - 4 - chip // 4)
    next_line = (away == 1) | (away == -1) | (away == 3) | (away == -3)
    far_line = (away == 2) | (away == -2)
    most = jnp.max(jnp.where(next_line, sums, 0.0)).astype(jnp.int32)
    most_far = jnp.max(jnp.where(far_line, sums, 0.0)).astype(jnp.int32)
    branch, cap = jnp.int32(len(CAPS) - 1), jnp.int32(CAPS[-1][0])
    for n in range(len(CAPS) - 2, -1, -1):
        enough = (most <= CAPS[n][0]) & (most_far <= CAPS[n][1])
        branch = jnp.where(enough, n, branch)
        cap = jnp.where(enough, CAPS[n][0], cap)
    which[0] = branch

    tp, tq, tt = split(tile)
    op, oq, ot = split(iota((64, 64), 1))
    placed = dot(ones((tq == oq) & (op * 4 + ot < tp * 4 + tt)), need)
    sp, sq, st = split(iota((64, 1), 0))
    entry = (sp * 4 + st).astype(F32)
    chip, slot = iota((64, 128), 1), iota((64, 128), 1).astype(F32)
    plan[...] = jnp.zeros_like(plan)
    for g, d in enumerate(DIST):
        other = (q + d) % RING
        there = chip == jnp.where(core == 0, p * 4 + other, other * 4 + p)
        wants = jnp.sum(jnp.where(there, need, 0.0), axis=1, keepdims=True)
        where = jnp.sum(jnp.where(there, placed, 0.0), axis=1, keepdims=True)
        taken = (wants > 0.0) & (sq == q) & (where == slot)
        plan[g : g + 1, :] = jnp.sum(jnp.where(taken, entry, 0.0), axis=0, keepdims=True).astype(jnp.int32)
    where = jnp.sum(jnp.where(chip == x * 4 + y, placed, 0.0), axis=1, keepdims=True)
    for k in range(4):
        source = sources[k : k + 1, :]
        tp, tq, tt = split(source)
        after = jnp.sum(jnp.where(source == tile, where, 0.0), axis=0, keepdims=True).astype(jnp.int32)
        live = counts[...] > k
        near = tq == q
        d = (tq - q + RING) % RING
        group = jnp.where(d == 1, 0, jnp.where(d == 3, 1, 2))
        plan[4 + k : 5 + k, 0:64] = jnp.where(live & near, tp * 4 + tt, p * 4)
        plan[8 + k : 9 + k, 0:64] = jnp.where(live & ~near, group * cap + after, 0)
        plan[12 + k : 13 + k, 0:64] = jnp.where(live & ~near, 0, 1)
        plan[16 + k : 17 + k, 0:64] = jnp.where(live, 1, 0)


def make_tables(sources, counts):
    smem, vmem = pl.BlockSpec(memory_space=pltpu.SMEM), pl.BlockSpec(memory_space=pltpu.VMEM)
    return pl.pallas_call(
        tables,
        out_shape=(jax.ShapeDtypeStruct((24, 128), jnp.int32), jax.ShapeDtypeStruct((1,), jnp.int32)),
        in_specs=[vmem, vmem],
        out_specs=(vmem, smem),
    )(sources.T, counts.reshape(1, -1))


def main(
    caps, width, plan, a_ref, b_ref, amp_ref, l_ref, eo_ref, ev_ref,
    res_ref, new_ref, norm_ref,
    abuf, bbuf, amps_mine, amps_away, ampbuf, lbuf, occ, cyc, row0, row1, row2, row3, packs, got0, got1, got2, got3,
    resbuf, resin, nacc, nbuf, ssem, rsem, lsem,
):
    core, p, q, x, y = place()
    z = lax.axis_index("occ")
    sister = 1 - core
    rows, got = (row0, row1, row2, row3), (got0, got1, got2, got3)
    half_k = width // 2
    relay = 3 * half_k // 2
    sizes = (caps[0], caps[0], caps[1])
    bases = (0, caps[0], 2 * caps[0])

    def at(fp, fq):
        fp, fq = fp % RING, fq % RING
        return (z, jnp.where(core == 0, (fp * 4 + fq) * 2, (fq * 4 + fp) * 2 + 1))

    def on_chip(zz, cc):
        return (zz, (x * 4 + y) * 2 + cc)

    group = [on_chip((z + dz) % 4, (core + dc) % 2) for dz in (2, 1, 3, 0) for dc in (1, 0) if dz or dc]
    plane = [at(p + dp, q + dq) for dp in (2, 1, 3, 0) for dq in (2, 1, 3, 0) if dp or dq]
    partners = group + plane
    barrier = pltpu.get_barrier_semaphore()
    for one in partners:
        pl.semaphore_signal(barrier, inc=1, device_id=one, device_id_type=MESH)

    made = {}

    def send(key, src, dst, dev):
        n = len(made)
        made[key] = pltpu.make_async_remote_copy(
            src_ref=src, dst_ref=dst, send_sem=ssem.at[n], recv_sem=rsem.at[n], device_id=dev, device_id_type=MESH
        )
        made[key].start()

    def arrived(key):
        made[key].wait_recv()

    own_b = pltpu.make_async_copy(b_ref, bbuf.at[core], lsem.at[0])
    own_l = pltpu.make_async_copy(l_ref, lbuf.at[core], lsem.at[1])
    own_b.start()
    own_l.start()

    for at_col in range(0, half_k, 1024):
        left = a_ref[:, at_col : at_col + 1024].astype(F32)
        right = a_ref[:, half_k + at_col : half_k + at_col + 1024].astype(F32)
        abuf[0, p, :, at_col : at_col + 1024] = left[:16].astype(BF16)
        abuf[0, p, :, half_k + at_col : half_k + at_col + 1024] = right[:16].astype(BF16)
        abuf[0, p, :, width + at_col : width + at_col + 1024] = jnp.concatenate([left[16:], right[16:]], axis=0).astype(BF16)

    pl.semaphore_wait(barrier, len(partners))

    halves = (pl.ds(0, relay), pl.ds(relay, relay))

    def along_first(way, h):
        send(("a1", way, h), abuf.at[0, p, :, halves[h]], abuf.at[0, p, :, halves[h]], at(p + way, q))

    def spread(i):
        pp = (p + i) % RING
        for n in range(2):
            send(("a2", i, 1, n), abuf.at[0, pp, :, halves[n]], abuf.at[3, pp, :, halves[n]], at(p, q + 1))
            m = 1 - n
            send(("a2", i, -1, m), abuf.at[0, pp, :, halves[m]], abuf.at[1, pp, :, halves[m]], at(p, q - 1))

    def pass_on(i):
        pp = (p + i) % RING
        arrived(("a2", i, 1, 0))
        send(("a2r", i, 1), abuf.at[3, pp, :, halves[0]], abuf.at[2, pp, :, halves[0]], at(p, q + 1))
        arrived(("a2", i, -1, 1))
        send(("a2r", i, -1), abuf.at[1, pp, :, halves[1]], abuf.at[2, pp, :, halves[1]], at(p, q - 1))

    along_first(1, 0)
    along_first(-1, 1)
    along_first(1, 1)
    along_first(-1, 0)
    to_sister = on_chip(z, sister)
    send("b", b_ref, bbuf.at[core], to_sister)
    send("l", l_ref, lbuf.at[core], to_sister)

    def amps_of(cc, keep):
        for fq in range(RING):
            for pair in range(0, RING, 2):
                tails = []
                for fp in (pair, pair + 1):
                    chip = fp * 4 + fq if cc == 0 else fq * 4 + fp
                    block = amp_ref[48 * chip : 48 * chip + 48, :].astype(F32)
                    block = block[24 * cc : 24 * cc + 24]
                    keep[fq, 16 * fp : 16 * fp + 16, :] = block[:16].astype(BF16)
                    tails.append(block[16:])
                keep[fq, 64 + 8 * pair : 80 + 8 * pair, :] = jnp.concatenate(tails, axis=0).astype(BF16)

    @pl.when(core == 0)
    def _():
        amps_of(0, amps_mine)
        amps_of(1, amps_away)

    @pl.when(core == 1)
    def _():
        amps_of(1, amps_mine)
        amps_of(0, amps_away)

    send("amp", amps_away, ampbuf, to_sister)

    pp, pm = (p + 1) % RING, (p + 3) % RING
    arrived(("a1", 1, 0))
    send(("a1r", 1), abuf.at[0, pm, :, halves[0]], abuf.at[0, pm, :, halves[0]], at(p + 1, q))
    arrived(("a1", -1, 1))
    send(("a1r", -1), abuf.at[0, pp, :, halves[1]], abuf.at[0, pp, :, halves[1]], at(p - 1, q))
    spread(0)
    for part in range(eo_ref.shape[0] // 128):
        values = jnp.broadcast_to(eo_ref[part * 128 : part * 128 + 128].reshape(1, 128), (128, 128))
        occ[part * 128 : part * 128 + 128, :] = values.T
    arrived(("a1", 1, 1))
    spread(3)
    arrived(("a1", -1, 0))
    spread(1)
    arrived(("a1r", 1))
    arrived(("a1r", -1))
    spread(2)

    def multiply(j, first, tiles):
        row = (q + j) % RING

        def one_tile(n, carry):
            cc = (core + n // 2) % 2
            t = cc * 2 + n % 2
            cols = pl.ds(pl.multiple_of((t % 2) * 256, 256), 256)

            def one_part(n, sums):
                start = pl.multiple_of(n * PART, PART)

                def block(first):
                    return abuf[j, :, :, pl.ds(first + start, PART)].reshape(64, PART)

                def product(first):
                    return jnp.dot(
                        jnp.concatenate([block(first), block(width)], axis=0), bbuf[cc, pl.ds(first + start, PART), cols],
                        preferred_element_type=F32,
                    )

                return sums[0] + product(0), sums[1] + product(half_k)

            zero = jnp.zeros((128, 256), F32)
            sum0, sum1 = lax.fori_loop(0, half_k // PART, one_part, (zero, zero))
            main_rows = sum0[:64] + sum1[:64]
            tail_rows = sum0[64:].reshape(4, 2, 8, 256)[:, 0] + sum1[64:].reshape(4, 2, 8, 256)[:, 1]
            cycle = jnp.concatenate([main_rows, tail_rows.reshape(32, 256)], axis=0).astype(BF16)
            cyc[j, t] = cycle
            amps = jnp.where(cc == core, amps_mine[row, :, cols].astype(F32), ampbuf[row, :, cols].astype(F32))
            rows[j][p * 4 + t] = (amps + cycle.astype(F32)).astype(BF16)
            return carry

        lax.fori_loop(first, first + tiles, one_tile, 0)

    def share(j, n):
        two = pl.ds(p * 4 + 2 * ((core + n) % 2), 2)
        for way in (1, -1):
            send(("e1", j, way, n), rows[j].at[two], rows[j].at[two], at(p + way, q))

    def share_on(j):
        for n, way, source in ((0, 1, pm), (1, -1, pp)):
            arrived(("e1", j, way, n))
            two = pl.ds(source * 4 + 2 * ((core + n) % 2), 2)
            send(("e1r", j, n), rows[j].at[two], rows[j].at[two], at(p + way, q))

    def hand_out(j):
        arrived(("e1", j, 1, 1))
        arrived(("e1", j, -1, 0))
        arrived(("e1r", j, 0))
        arrived(("e1r", j, 1))
        for g in (2, 0, 1):
            d = DIST[g]

            def one_slot(s, carry, g=g):
                packs[j, bases[g] + s] = rows[j][plan[g, s]]
                return carry

            lax.fori_loop(0, sizes[g], one_slot, 0)
            there = DIST.index((-d) % RING)
            send(
                ("e2", j, g), packs.at[j, pl.ds(bases[g], sizes[g])],
                got[(j - d) % RING].at[pl.ds(bases[there], sizes[there])], at(p, q + d),
            )

    pass_on(0)
    own_b.wait()
    arrived("amp")
    multiply(0,0,2)
    pass_on(3)
    arrived("b")
    multiply(0,2,2)
    pass_on(1)
    own_l.wait()
    arrived("l")
    mine = (x * 4 + y) * 4

    def mask_weights(s, carry):
        t, k = s // 4, s % 4
        slot = (t % 2) * 4 + k
        lbuf[t // 2, slot] = lbuf[t // 2, slot] * plan[16 + k, mine + t].astype(F32).astype(BF16)
        return carry

    lax.fori_loop(0, 16, mask_weights, 0)
    pass_on(2)
    share(0, 0)
    share(0, 1)
    for i in range(RING):
        arrived(("a2", i, 1, 1))
    multiply(3,0,4)
    share(3, 0)
    share(3, 1)
    share_on(0)
    for i in range(RING):
        arrived(("a2", i, -1, 0))
    multiply(1,0,4)
    share(1, 0)
    share(1, 1)
    share_on(3)
    share_on(1)
    for i in range(RING):
        arrived(("a2r", i, 1))
        arrived(("a2r", i, -1))
    hand_out(0)
    multiply(2,0,2)
    share(2,0)
    multiply(2,2,2)
    share(2,1)
    hand_out(3)
    hand_out(1)
    share_on(2)
    hand_out(2)

    nacc[...] = jnp.zeros_like(nacc)

    def finish(j):
        for g, d in enumerate(DIST):
            arrived(("e2", (j - d) % RING, DIST.index((-d) % RING)))
        row = (q + j) % RING

        def one_tile(t, carry):
            cols = pl.ds(pl.multiple_of((t % 2) * 256, 256), 256)
            total = jnp.zeros((96, 256), F32)
            for k in range(4):
                near = rows[j][plan[4 + k, mine + t]].astype(F32)
                far = got[j][plan[8 + k, mine + t]].astype(F32)
                block = jnp.where(plan[12 + k, mine + t] == 1, near, far).astype(BF16)
                total += jnp.dot(block, lbuf[t // 2, (t % 2) * 4 + k], preferred_element_type=F32)
            residual = (total + cyc[j, t].astype(F32)).astype(BF16)
            wide = residual.astype(F32)
            resbuf[t // 2, row, :, cols] = residual
            nacc[...] += (wide * wide).reshape(12, 8, 256).sum(axis=0)
            return carry

        lax.fori_loop(0, 4, one_tile, 0)
        send(("res", j), resbuf.at[sister, row], resin.at[row], to_sister)

    for j in (2, 0, 3, 1):
        finish(j)

    def write(first, last):
        def rows_of(cc, fq, fp):
            pair = 64 + 16 * (fp // 2)
            head = jnp.where(core == cc, resbuf[cc, fq, 16 * fp : 16 * fp + 16, :].astype(F32), resin[fq, 16 * fp : 16 * fp + 16, :].astype(F32))
            tail = jnp.where(core == cc, resbuf[cc, fq, pair : pair + 16, :].astype(F32), resin[fq, pair : pair + 16, :].astype(F32))
            return [head, tail[8 * (fp % 2) : 8 * (fp % 2) + 8]]

        for chip in range(first, last):
            fx, fy = chip // 4, chip % 4
            block = jnp.concatenate(rows_of(0, fy, fx) + rows_of(1, fx, fy), axis=0)
            here = slice(48 * chip, 48 * chip + 48)
            lanes = occ[here, :]
            denom = jnp.concatenate([lanes] * (block.shape[1] // 128), axis=1) + ev_ref[...]
            res_ref[here, :] = block.astype(BF16)
            new_ref[here, :] = (amp_ref[here, :].astype(F32) - block / denom).astype(BF16)

    def spread_norm(stage, slot, value, devices):
        nbuf[stage, slot] = jnp.full((8, 128), value, F32)
        for n, dev in enumerate(devices):
            send(("n", stage, n), nbuf.at[stage, slot], nbuf.at[stage, slot], dev)

    def sum_norm(stage, devices):
        for n in range(len(devices)):
            arrived(("n", stage, n))
        total = nbuf[stage, 0]
        for n in range(1, len(devices) + 1):
            total = total + nbuf[stage, n]
        return jnp.max(total)

    spread_norm(0, z * 2 + core, jnp.sum(nacc[...]), group)
    for j in range(RING):
        arrived(("res", j))
    write(0, 8)
    spread_norm(1, p * 4 + q, sum_norm(0, group), plane)
    write(8, 16)
    norm_ref[0] = sum_norm(1, plane)
    for one in made.values():
        one.wait_send()


COPIES = 96


def run_main(caps, number, plan, a, b, amp, blocks, eo, ev):
    width, columns = b.shape
    rows = amp.shape[0] // 8
    smem, vmem = pl.BlockSpec(memory_space=pltpu.SMEM), pl.BlockSpec(memory_space=pltpu.VMEM)
    anywhere = pl.BlockSpec(memory_space=pl.ANY)
    out = jax.ShapeDtypeStruct(amp.shape, BF16)
    row_buf = pltpu.VMEM((16, rows, 256), BF16)
    got_buf = pltpu.VMEM((2 * caps[0] + caps[1], rows, 256), BF16)
    part = pltpu.VMEM((RING, rows, columns), BF16)
    return pl.pallas_call(
        functools.partial(main, caps, width),
        out_shape=(out, out, jax.ShapeDtypeStruct((1,), F32)),
        in_specs=[smem, vmem, anywhere, vmem, anywhere, vmem, vmem],
        out_specs=(vmem, vmem, smem),
        scratch_shapes=[
            pltpu.VMEM((RING, RING, 16, width + width // 2), BF16),
            pltpu.VMEM((2, width, columns), BF16),
            part, part, part,
            pltpu.VMEM((2, 8, 256, 256), BF16),
            pltpu.VMEM((amp.shape[0], 128), F32),
            pltpu.VMEM((RING, 4, rows, 256), BF16),
            row_buf, row_buf, row_buf, row_buf,
            pltpu.VMEM((RING, 2 * caps[0] + caps[1], rows, 256), BF16),
            got_buf, got_buf, got_buf, got_buf,
            pltpu.VMEM((2, RING, rows, columns), BF16),
            part,
            pltpu.VMEM((8, 256), F32),
            pltpu.VMEM((2, 16, 8, 128), F32),
            pltpu.SemaphoreType.DMA((COPIES,)),
            pltpu.SemaphoreType.DMA((COPIES,)),
            pltpu.SemaphoreType.DMA((2,)),
        ],
        compiler_params=pltpu.CompilerParams(
            collective_id=number, has_side_effects=True, vmem_limit_bytes=60 * 2**20
        ),
        cost_estimate=pl.CostEstimate(flops=8 * 10**9, bytes_accessed=20 * 2**20, transcendentals=0),
    )(plan, a, b, amp, blocks, eo, ev)


def on_device(amps, cycle_amps, cycle_ints, ladder_ints, sources, counts, eps_occ, eps_vir):
    plan, which = make_tables(sources, counts)
    blocks = ladder_ints.reshape(8, *ladder_ints.shape[2:])
    branches = [functools.partial(run_main, caps, n) for n, caps in enumerate(CAPS)]
    residual, new_amps, norm = lax.switch(
        which[0], branches, plan, cycle_amps, cycle_ints, amps, blocks, eps_occ, eps_vir.reshape(1, -1)
    )
    return residual, new_amps, norm[0]


def solution(mesh):
    placed = (
        P("occ", "vir"),
        P(("occ", "vir"), None),
        P(None, "vir"),
        P("vir", None, None, None),
        P(),
        P(),
        P("occ"),
        P("vir"),
    )
    return jax.shard_map(
        on_device,
        mesh=mesh,
        in_specs=placed,
        out_specs=(P("occ", "vir"), P("occ", "vir"), P()),
        check_vma=False,
    )
```

```python
import functools

import jax
import jax.numpy as jnp
from jax import lax
from jax.experimental import pallas as pl
from jax.experimental.pallas import tpu as pltpu
from jax.sharding import PartitionSpec as P

MESH = pl.DeviceIdType.MESH
RING = 4
DIST = (1, 3, 2)
CAPS = ((5, 5), (6, 5), (6, 6), (8, 8), (16, 16))
PART = 2048
F32, BF16 = jnp.float32, jnp.bfloat16


def place():
    vir = lax.axis_index("vir")
    core = vir % 2
    y = (vir // 2) % RING
    x = vir // (2 * RING)
    first = jnp.where(core == 0, x, y)
    second = jnp.where(core == 0, y, x)
    return core, first, second, x, y


def tables(sources, counts, plan, which):
    core, p, q, x, y = place()

    def iota(shape, axis):
        return lax.broadcasted_iota(jnp.int32, shape, axis)

    def ones(mask):
        return jnp.where(mask, 1.0, 0.0)

    def dot(one, other):
        return jnp.dot(one.astype(BF16), other.astype(BF16), preferred_element_type=F32)

    def split(tile):
        tx, ty = tile // 16, (tile // 4) % 4
        return jnp.where(core == 0, tx, ty), jnp.where(core == 0, ty, tx), tile % 4

    tile = iota((64, 64), 0)
    hits = jnp.zeros((64, 64), F32)
    for k in range(4):
        hits += ones((sources[k : k + 1, :] == tile) & (counts[...] > k))
    need = jnp.minimum(dot(hits, ones(iota((64, 128), 0) // 4 == iota((64, 128), 1))), 1.0)

    line, member = iota((16, 64), 0), iota((16, 64), 1)
    inside = ((line < 4) & ((member // 4) % 4 == line)) | ((line >= 4) & (line < 8) & (member // 16 == line - 4))
    line, chip = iota((16, 128), 0), iota((16, 128), 1)
    sums = dot(ones(inside), need)
    away = jnp.where(line < 4, line - chip % 4, line - 4 - chip // 4)
    next_line = (away == 1) | (away == -1) | (away == 3) | (away == -3)
    far_line = (away == 2) | (away == -2)
    most = jnp.max(jnp.where(next_line, sums, 0.0)).astype(jnp.int32)
    most_far = jnp.max(jnp.where(far_line, sums, 0.0)).astype(jnp.int32)
    branch, cap = jnp.int32(len(CAPS) - 1), jnp.int32(CAPS[-1][0])
    for n in range(len(CAPS) - 2, -1, -1):
        enough = (most <= CAPS[n][0]) & (most_far <= CAPS[n][1])
        branch = jnp.where(enough, n, branch)
        cap = jnp.where(enough, CAPS[n][0], cap)
    which[0] = branch

    tp, tq, tt = split(tile)
    op, oq, ot = split(iota((64, 64), 1))
    placed = dot(ones((tq == oq) & (op * 4 + ot < tp * 4 + tt)), need)
    sp, sq, st = split(iota((64, 1), 0))
    entry = (sp * 4 + st).astype(F32)
    chip, slot = iota((64, 128), 1), iota((64, 128), 1).astype(F32)
    plan[...] = jnp.zeros_like(plan)
    for g, d in enumerate(DIST):
        other = (q + d) % RING
        there = chip == jnp.where(core == 0, p * 4 + other, other * 4 + p)
        wants = jnp.sum(jnp.where(there, need, 0.0), axis=1, keepdims=True)
        where = jnp.sum(jnp.where(there, placed, 0.0), axis=1, keepdims=True)
        taken = (wants > 0.0) & (sq == q) & (where == slot)
        plan[g : g + 1, :] = jnp.sum(jnp.where(taken, entry, 0.0), axis=0, keepdims=True).astype(jnp.int32)
    where = jnp.sum(jnp.where(chip == x * 4 + y, placed, 0.0), axis=1, keepdims=True)
    for k in range(4):
        source = sources[k : k + 1, :]
        tp, tq, tt = split(source)
        after = jnp.sum(jnp.where(source == tile, where, 0.0), axis=0, keepdims=True).astype(jnp.int32)
        live = counts[...] > k
        near = tq == q
        d = (tq - q + RING) % RING
        group = jnp.where(d == 1, 0, jnp.where(d == 3, 1, 2))
        plan[4 + k : 5 + k, 0:64] = jnp.where(live & near, tp * 4 + tt, p * 4)
        plan[8 + k : 9 + k, 0:64] = jnp.where(live & ~near, group * cap + after, 0)
        plan[12 + k : 13 + k, 0:64] = jnp.where(live & ~near, 0, 1)
        plan[16 + k : 17 + k, 0:64] = jnp.where(live, 1, 0)


def make_tables(sources, counts):
    smem, vmem = pl.BlockSpec(memory_space=pltpu.SMEM), pl.BlockSpec(memory_space=pltpu.VMEM)
    return pl.pallas_call(
        tables,
        out_shape=(jax.ShapeDtypeStruct((24, 128), jnp.int32), jax.ShapeDtypeStruct((1,), jnp.int32)),
        in_specs=[vmem, vmem],
        out_specs=(vmem, smem),
    )(sources.T, counts.reshape(1, -1))


def main(
    caps, width, plan, a_ref, b_ref, amp_ref, l_ref, eo_ref, ev_ref,
    res_ref, new_ref, norm_ref,
    abuf, bbuf, amps_mine, amps_away, ampbuf, lbuf, occ, cyc, row0, row1, row2, row3, packs, got0, got1, got2, got3,
    resbuf, resin, nacc, nbuf, ssem, rsem, lsem,
):
    core, p, q, x, y = place()
    z = lax.axis_index("occ")
    sister = 1 - core
    rows, got = (row0, row1, row2, row3), (got0, got1, got2, got3)
    half_k = width // 2
    relay = 3 * half_k // 2
    sizes = (caps[0], caps[0], caps[1])
    bases = (0, caps[0], 2 * caps[0])

    def at(fp, fq):
        fp, fq = fp % RING, fq % RING
        return (z, jnp.where(core == 0, (fp * 4 + fq) * 2, (fq * 4 + fp) * 2 + 1))

    def on_chip(zz, cc):
        return (zz, (x * 4 + y) * 2 + cc)

    group = [on_chip((z + dz) % 4, (core + dc) % 2) for dz in (2, 1, 3, 0) for dc in (1, 0) if dz or dc]
    plane = [at(p + dp, q + dq) for dp in (2, 1, 3, 0) for dq in (2, 1, 3, 0) if dp or dq]
    partners = group + plane
    barrier = pltpu.get_barrier_semaphore()
    for one in partners:
        pl.semaphore_signal(barrier, inc=1, device_id=one, device_id_type=MESH)

    made = {}

    def send(key, src, dst, dev):
        n = len(made)
        made[key] = pltpu.make_async_remote_copy(
            src_ref=src, dst_ref=dst, send_sem=ssem.at[n], recv_sem=rsem.at[n], device_id=dev, device_id_type=MESH
        )
        made[key].start()

    def arrived(key):
        made[key].wait_recv()

    own_b = pltpu.make_async_copy(b_ref, bbuf.at[core], lsem.at[0])
    own_l = pltpu.make_async_copy(l_ref, lbuf.at[core], lsem.at[1])
    own_b.start()
    own_l.start()

    for at_col in range(0, half_k, 1024):
        left = a_ref[:, at_col : at_col + 1024].astype(F32)
        right = a_ref[:, half_k + at_col : half_k + at_col + 1024].astype(F32)
        abuf[0, p, :, at_col : at_col + 1024] = left[:16].astype(BF16)
        abuf[0, p, :, half_k + at_col : half_k + at_col + 1024] = right[:16].astype(BF16)
        abuf[0, p, :, width + at_col : width + at_col + 1024] = jnp.concatenate([left[16:], right[16:]], axis=0).astype(BF16)

    pl.semaphore_wait(barrier, len(partners))

    halves = (pl.ds(0, relay), pl.ds(relay, relay))

    def along_first(way, h):
        send(("a1", way, h), abuf.at[0, p, :, halves[h]], abuf.at[0, p, :, halves[h]], at(p + way, q))

    def spread(i):
        pp = (p + i) % RING
        for n in range(2):
            send(("a2", i, 1, n), abuf.at[0, pp, :, halves[n]], abuf.at[3, pp, :, halves[n]], at(p, q + 1))
            m = 1 - n
            send(("a2", i, -1, m), abuf.at[0, pp, :, halves[m]], abuf.at[1, pp, :, halves[m]], at(p, q - 1))

    def pass_on(i):
        pp = (p + i) % RING
        arrived(("a2", i, 1, 0))
        send(("a2r", i, 1), abuf.at[3, pp, :, halves[0]], abuf.at[2, pp, :, halves[0]], at(p, q + 1))
        arrived(("a2", i, -1, 1))
        send(("a2r", i, -1), abuf.at[1, pp, :, halves[1]], abuf.at[2, pp, :, halves[1]], at(p, q - 1))

    along_first(1, 0)
    along_first(-1, 1)
    along_first(1, 1)
    along_first(-1, 0)
    to_sister = on_chip(z, sister)
    send("b", b_ref, bbuf.at[core], to_sister)
    send("l", l_ref, lbuf.at[core], to_sister)

    def amps_of(cc, keep):
        for fq in range(RING):
            for pair in range(0, RING, 2):
                tails = []
                for fp in (pair, pair + 1):
                    chip = fp * 4 + fq if cc == 0 else fq * 4 + fp
                    block = amp_ref[48 * chip : 48 * chip + 48, :].astype(F32)
                    block = block[24 * cc : 24 * cc + 24]
                    keep[fq, 16 * fp : 16 * fp + 16, :] = block[:16].astype(BF16)
                    tails.append(block[16:])
                keep[fq, 64 + 8 * pair : 80 + 8 * pair, :] = jnp.concatenate(tails, axis=0).astype(BF16)

    @pl.when(core == 0)
    def _():
        amps_of(0, amps_mine)
        amps_of(1, amps_away)

    @pl.when(core == 1)
    def _():
        amps_of(1, amps_mine)
        amps_of(0, amps_away)

    send("amp", amps_away, ampbuf, to_sister)

    pp, pm = (p + 1) % RING, (p + 3) % RING
    arrived(("a1", 1, 0))
    send(("a1r", 1), abuf.at[0, pm, :, halves[0]], abuf.at[0, pm, :, halves[0]], at(p + 1, q))
    arrived(("a1", -1, 1))
    send(("a1r", -1), abuf.at[0, pp, :, halves[1]], abuf.at[0, pp, :, halves[1]], at(p - 1, q))
    spread(0)
    for part in range(eo_ref.shape[0] // 128):
        values = jnp.broadcast_to(eo_ref[part * 128 : part * 128 + 128].reshape(1, 128), (128, 128))
        occ[part * 128 : part * 128 + 128, :] = values.T
    arrived(("a1", 1, 1))
    spread(3)
    arrived(("a1", -1, 0))
    spread(1)
    arrived(("a1r", 1))
    arrived(("a1r", -1))
    spread(2)

    def multiply(j, first, tiles):
        row = (q + j) % RING

        def one_tile(n, carry):
            cc = (core + n // 2) % 2
            t = cc * 2 + n % 2
            cols = pl.ds(pl.multiple_of((t % 2) * 256, 256), 256)

            def one_part(n, sums):
                start = pl.multiple_of(n * PART, PART)

                def block(first):
                    return abuf[j, :, :, pl.ds(first + start, PART)].reshape(64, PART)

                def product(first):
                    return jnp.dot(
                        jnp.concatenate([block(first), block(width)], axis=0), bbuf[cc, pl.ds(first + start, PART), cols],
                        preferred_element_type=F32,
                    )

                return sums[0] + product(0), sums[1] + product(half_k)

            zero = jnp.zeros((128, 256), F32)
            sum0, sum1 = lax.fori_loop(0, half_k // PART, one_part, (zero, zero))
            main_rows = sum0[:64] + sum1[:64]
            tail_rows = sum0[64:].reshape(4, 2, 8, 256)[:, 0] + sum1[64:].reshape(4, 2, 8, 256)[:, 1]
            cycle = jnp.concatenate([main_rows, tail_rows.reshape(32, 256)], axis=0).astype(BF16)
            cyc[j, t] = cycle
            amps = jnp.where(cc == core, amps_mine[row, :, cols].astype(F32), ampbuf[row, :, cols].astype(F32))
            rows[j][p * 4 + t] = (amps + cycle.astype(F32)).astype(BF16)
            return carry

        lax.fori_loop(first, first + tiles, one_tile, 0)

    def share(j, n):
        two = pl.ds(p * 4 + 2 * ((core + n) % 2), 2)
        for way in (1, -1):
            send(("e1", j, way, n), rows[j].at[two], rows[j].at[two], at(p + way, q))

    def share_on(j):
        for n, way, source in ((0, 1, pm), (1, -1, pp)):
            arrived(("e1", j, way, n))
            two = pl.ds(source * 4 + 2 * ((core + n) % 2), 2)
            send(("e1r", j, n), rows[j].at[two], rows[j].at[two], at(p + way, q))

    def hand_out(j):
        arrived(("e1", j, 1, 1))
        arrived(("e1", j, -1, 0))
        arrived(("e1r", j, 0))
        arrived(("e1r", j, 1))
        for g in (2, 0, 1):
            d = DIST[g]

            def one_slot(s, carry, g=g):
                packs[j, bases[g] + s] = rows[j][plan[g, s]]
                return carry

            lax.fori_loop(0, sizes[g], one_slot, 0)
            there = DIST.index((-d) % RING)
            send(
                ("e2", j, g), packs.at[j, pl.ds(bases[g], sizes[g])],
                got[(j - d) % RING].at[pl.ds(bases[there], sizes[there])], at(p, q + d),
            )

    pass_on(0)
    own_b.wait()
    arrived("amp")
    multiply(0, 0, 2)
    pass_on(3)
    arrived("b")
    multiply(0, 2, 2)
    pass_on(1)
    own_l.wait()
    arrived("l")
    mine = (x * 4 + y) * 4

    def mask_weights(s, carry):
        t, k = s // 4, s % 4
        slot = (t % 2) * 4 + k
        lbuf[t // 2, slot] = lbuf[t // 2, slot] * plan[16 + k, mine + t].astype(F32).astype(BF16)
        return carry

    lax.fori_loop(0, 16, mask_weights, 0)
    pass_on(2)
    share(0, 0)
    share(0, 1)
    for i in range(RING):
        arrived(("a2", i, 1, 1))
    multiply(3, 0, 2)
    share(3, 0)
    multiply(3, 2, 2)
    share(3, 1)
    share_on(0)
    for i in range(RING):
        arrived(("a2", i, -1, 0))
    multiply(1, 0, 2)
    share(1, 0)
    multiply(1, 2, 2)
    share(1, 1)
    share_on(3)
    share_on(1)
    for i in range(RING):
        arrived(("a2r", i, 1))
        arrived(("a2r", i, -1))
    hand_out(0)
    multiply(2, 0, 2)
    share(2, 0)
    multiply(2, 2, 2)
    share(2, 1)
    hand_out(3)
    hand_out(1)
    share_on(2)
    hand_out(2)

    nacc[...] = jnp.zeros_like(nacc)

    def finish(*chunks):
        for j in chunks:
            for g, d in enumerate(DIST):
                arrived(("e2", (j - d) % RING, DIST.index((-d) % RING)))

        def one_tile(t, carry):
            cols = pl.ds(pl.multiple_of((t % 2) * 256, 256), 256)
            total = jnp.zeros((96 * len(chunks), 256), F32)
            for k in range(4):
                parts = []
                for j in chunks:
                    near = rows[j][plan[4 + k, mine + t]].astype(F32)
                    far = got[j][plan[8 + k, mine + t]].astype(F32)
                    parts.append(jnp.where(plan[12 + k, mine + t] == 1, near, far).astype(BF16))
                block = jnp.concatenate(parts, axis=0)
                total += jnp.dot(block, lbuf[t // 2, (t % 2) * 4 + k], preferred_element_type=F32)
            for n, j in enumerate(chunks):
                residual = (total[96 * n : 96 * n + 96] + cyc[j, t].astype(F32)).astype(BF16)
                wide = residual.astype(F32)
                resbuf[t // 2, (q + j) % RING, :, cols] = residual
                nacc[...] += (wide * wide).reshape(12, 8, 256).sum(axis=0)
            return carry

        lax.fori_loop(0, 4, one_tile, 0)
        for j in chunks:
            row = (q + j) % RING
            send(("res", j), resbuf.at[sister, row], resin.at[row], to_sister)

    finish(2)
    finish(0, 3, 1)

    def write(first, last):
        def rows_of(cc, fq, fp):
            pair = 64 + 16 * (fp // 2)
            head = jnp.where(core == cc, resbuf[cc, fq, 16 * fp : 16 * fp + 16, :].astype(F32), resin[fq, 16 * fp : 16 * fp + 16, :].astype(F32))
            tail = jnp.where(core == cc, resbuf[cc, fq, pair : pair + 16, :].astype(F32), resin[fq, pair : pair + 16, :].astype(F32))
            return [head, tail[8 * (fp % 2) : 8 * (fp % 2) + 8]]

        for chip in range(first, last):
            fx, fy = chip // 4, chip % 4
            block = jnp.concatenate(rows_of(0, fy, fx) + rows_of(1, fx, fy), axis=0)
            here = slice(48 * chip, 48 * chip + 48)
            lanes = occ[here, :]
            denom = jnp.concatenate([lanes] * (block.shape[1] // 128), axis=1) + ev_ref[...]
            res_ref[here, :] = block.astype(BF16)
            new_ref[here, :] = (amp_ref[here, :].astype(F32) - block / denom).astype(BF16)

    def spread_norm(stage, slot, value, devices):
        nbuf[stage, slot] = value
        for n, dev in enumerate(devices):
            send(("n", stage, n), nbuf.at[stage, slot], nbuf.at[stage, slot], dev)

    def sum_norm(stage, devices):
        for n in range(len(devices)):
            arrived(("n", stage, n))
        total = nbuf[stage, 0]
        for n in range(1, len(devices) + 1):
            total = total + nbuf[stage, n]
        return total

    earlier = list(made.values())
    spread_norm(0, z * 2 + core, nacc[:, 0:128] + nacc[:, 128:256], group)
    for j in range(RING):
        arrived(("res", j))
    write(0, 8)
    for one in earlier:
        one.wait_send()
    spread_norm(1, p * 4 + q, sum_norm(0, group), plane)
    write(8, 16)
    norm_ref[0] = jnp.sum(sum_norm(1, plane))
    for one in list(made.values())[len(earlier) :]:
        one.wait_send()


COPIES = 96


def run_main(caps, number, plan, a, b, amp, blocks, eo, ev):
    width, columns = b.shape
    rows = amp.shape[0] // 8
    smem, vmem = pl.BlockSpec(memory_space=pltpu.SMEM), pl.BlockSpec(memory_space=pltpu.VMEM)
    anywhere = pl.BlockSpec(memory_space=pl.ANY)
    out = jax.ShapeDtypeStruct(amp.shape, BF16)
    row_buf = pltpu.VMEM((16, rows, 256), BF16)
    got_buf = pltpu.VMEM((2 * caps[0] + caps[1], rows, 256), BF16)
    part = pltpu.VMEM((RING, rows, columns), BF16)
    return pl.pallas_call(
        functools.partial(main, caps, width),
        out_shape=(out, out, jax.ShapeDtypeStruct((1,), F32)),
        in_specs=[smem, vmem, anywhere, vmem, anywhere, vmem, vmem],
        out_specs=(vmem, vmem, smem),
        scratch_shapes=[
            pltpu.VMEM((RING, RING, 16, width + width // 2), BF16),
            pltpu.VMEM((2, width, columns), BF16),
            part, part, part,
            pltpu.VMEM((2, 8, 256, 256), BF16),
            pltpu.VMEM((amp.shape[0], 128), F32),
            pltpu.VMEM((RING, 4, rows, 256), BF16),
            row_buf, row_buf, row_buf, row_buf,
            pltpu.VMEM((RING, 2 * caps[0] + caps[1], rows, 256), BF16),
            got_buf, got_buf, got_buf, got_buf,
            pltpu.VMEM((2, RING, rows, columns), BF16),
            part,
            pltpu.VMEM((8, 256), F32),
            pltpu.VMEM((2, 16, 8, 128), F32),
            pltpu.SemaphoreType.DMA((COPIES,)),
            pltpu.SemaphoreType.DMA((COPIES,)),
            pltpu.SemaphoreType.DMA((2,)),
        ],
        compiler_params=pltpu.CompilerParams(
            collective_id=number, has_side_effects=True, vmem_limit_bytes=60 * 2**20
        ),
        cost_estimate=pl.CostEstimate(flops=8 * 10**9, bytes_accessed=20 * 2**20, transcendentals=0),
    )(plan, a, b, amp, blocks, eo, ev)


def on_device(amps, cycle_amps, cycle_ints, ladder_ints, sources, counts, eps_occ, eps_vir):
    plan, which = make_tables(sources, counts)
    blocks = ladder_ints.reshape(8, *ladder_ints.shape[2:])
    branches = [functools.partial(run_main, caps, n) for n, caps in enumerate(CAPS)]
    residual, new_amps, norm = lax.switch(
        which[0], branches, plan, cycle_amps, cycle_ints, amps, blocks, eps_occ, eps_vir.reshape(1, -1)
    )
    return residual, new_amps, norm[0]


def solution(mesh):
    placed = (
        P("occ", "vir"),
        P(("occ", "vir"), None),
        P(None, "vir"),
        P("vir", None, None, None),
        P(),
        P(),
        P("occ"),
        P("vir"),
    )
    return jax.shard_map(
        on_device,
        mesh=mesh,
        in_specs=placed,
        out_specs=(P("occ", "vir"), P("occ", "vir"), P()),
        check_vma=False,
    )
```

```python
import functools

import jax
import jax.numpy as jnp
from jax import lax
from jax.experimental import pallas as pl
from jax.experimental.pallas import tpu as pltpu
from jax.sharding import PartitionSpec as P

MESH = pl.DeviceIdType.MESH
RING = 4
DIST = (1, 3, 2)
CAPS = ((5, 5), (6, 5), (6, 6), (7, 7), (8, 8), (16, 16))
PART = 2048
F32, BF16 = jnp.float32, jnp.bfloat16


def place():
    vir = lax.axis_index("vir")
    core = vir % 2
    y = (vir // 2) % RING
    x = vir // (2 * RING)
    first = jnp.where(core == 0, x, y)
    second = jnp.where(core == 0, y, x)
    return core, first, second, x, y


def tables(sources, counts, plan, which):
    core, p, q, x, y = place()

    def iota(shape, axis):
        return lax.broadcasted_iota(jnp.int32, shape, axis)

    def ones(mask):
        return jnp.where(mask, 1.0, 0.0)

    def dot(one, other):
        return jnp.dot(one.astype(BF16), other.astype(BF16), preferred_element_type=F32)

    def split(tile):
        tx, ty = tile // 16, (tile // 4) % 4
        return jnp.where(core == 0, tx, ty), jnp.where(core == 0, ty, tx), tile % 4

    tile = iota((64, 64), 0)
    hits = jnp.zeros((64, 64), F32)
    for k in range(4):
        hits += ones((sources[k : k + 1, :] == tile) & (counts[...] > k))
    need = jnp.minimum(dot(hits, ones(iota((64, 128), 0) // 4 == iota((64, 128), 1))), 1.0)

    line, member = iota((16, 64), 0), iota((16, 64), 1)
    inside = ((line < 4) & ((member // 4) % 4 == line)) | ((line >= 4) & (line < 8) & (member // 16 == line - 4))
    line, chip = iota((16, 128), 0), iota((16, 128), 1)
    sums = dot(ones(inside), need)
    away = jnp.where(line < 4, line - chip % 4, line - 4 - chip // 4)
    next_line = (away == 1) | (away == -1) | (away == 3) | (away == -3)
    far_line = (away == 2) | (away == -2)
    most = jnp.max(jnp.where(next_line, sums, 0.0)).astype(jnp.int32)
    most_far = jnp.max(jnp.where(far_line, sums, 0.0)).astype(jnp.int32)
    branch, cap = jnp.int32(len(CAPS) - 1), jnp.int32(CAPS[-1][0])
    for n in range(len(CAPS) - 2, -1, -1):
        enough = (most <= CAPS[n][0]) & (most_far <= CAPS[n][1])
        branch = jnp.where(enough, n, branch)
        cap = jnp.where(enough, CAPS[n][0], cap)
    which[0] = branch

    tp, tq, tt = split(tile)
    op, oq, ot = split(iota((64, 64), 1))
    placed = dot(ones((tq == oq) & (op * 4 + ot < tp * 4 + tt)), need)
    sp, sq, st = split(iota((64, 1), 0))
    entry = (sp * 4 + st).astype(F32)
    chip, slot = iota((64, 128), 1), iota((64, 128), 1).astype(F32)
    plan[...] = jnp.zeros_like(plan)
    for g, d in enumerate(DIST):
        other = (q + d) % RING
        there = chip == jnp.where(core == 0, p * 4 + other, other * 4 + p)
        wants = jnp.sum(jnp.where(there, need, 0.0), axis=1, keepdims=True)
        where = jnp.sum(jnp.where(there, placed, 0.0), axis=1, keepdims=True)
        taken = (wants > 0.0) & (sq == q) & (where == slot)
        plan[g : g + 1, :] = jnp.sum(jnp.where(taken, entry, 0.0), axis=0, keepdims=True).astype(jnp.int32)
    where = jnp.sum(jnp.where(chip == x * 4 + y, placed, 0.0), axis=1, keepdims=True)
    for k in range(4):
        source = sources[k : k + 1, :]
        tp, tq, tt = split(source)
        after = jnp.sum(jnp.where(source == tile, where, 0.0), axis=0, keepdims=True).astype(jnp.int32)
        live = counts[...] > k
        near = tq == q
        d = (tq - q + RING) % RING
        group = jnp.where(d == 1, 0, jnp.where(d == 3, 1, 2))
        plan[4 + k : 5 + k, 0:64] = jnp.where(live & near, tp * 4 + tt, p * 4)
        plan[8 + k : 9 + k, 0:64] = jnp.where(live & ~near, group * cap + after, 0)
        plan[12 + k : 13 + k, 0:64] = jnp.where(live & ~near, 0, 1)
        plan[16 + k : 17 + k, 0:64] = jnp.where(live, 1, 0)


def make_tables(sources, counts):
    smem, vmem = pl.BlockSpec(memory_space=pltpu.SMEM), pl.BlockSpec(memory_space=pltpu.VMEM)
    return pl.pallas_call(
        tables,
        out_shape=(jax.ShapeDtypeStruct((24, 128), jnp.int32), jax.ShapeDtypeStruct((1,), jnp.int32)),
        in_specs=[vmem, vmem],
        out_specs=(vmem, smem),
    )(sources.T, counts.reshape(1, -1))


def main(
    caps, width, plan, a_ref, b_ref, amp_ref, l_ref, eo_ref, ev_ref,
    res_ref, new_ref, norm_ref,
    abuf, bbuf, amps_mine, amps_away, ampbuf, lbuf, occ, cyc, row0, row1, row2, row3, packs, got0, got1, got2, got3,
    resbuf, resin, nacc, nbuf, ssem, rsem, lsem,
):
    core, p, q, x, y = place()
    z = lax.axis_index("occ")
    sister = 1 - core
    rows, got = (row0, row1, row2, row3), (got0, got1, got2, got3)
    half_k = width // 2
    relay = 3 * half_k // 2
    sizes = (caps[0], caps[0], caps[1])
    bases = (0, caps[0], 2 * caps[0])

    def at(fp, fq):
        fp, fq = fp % RING, fq % RING
        return (z, jnp.where(core == 0, (fp * 4 + fq) * 2, (fq * 4 + fp) * 2 + 1))

    def on_chip(zz, cc):
        return (zz, (x * 4 + y) * 2 + cc)

    group = [on_chip((z + dz) % 4, (core + dc) % 2) for dz in (2, 1, 3, 0) for dc in (1, 0) if dz or dc]
    plane = [at(p + dp, q + dq) for dp in (2, 1, 3, 0) for dq in (2, 1, 3, 0) if dp or dq]
    partners = group + plane
    barrier = pltpu.get_barrier_semaphore()
    for one in partners:
        pl.semaphore_signal(barrier, inc=1, device_id=one, device_id_type=MESH)

    made = {}

    def describe(n, src, dst, dev):
        return pltpu.make_async_remote_copy(
            src_ref=src, dst_ref=dst, send_sem=ssem.at[n], recv_sem=rsem.at[n], device_id=dev, device_id_type=MESH
        )

    def send(key, src, dst, dev):
        made[key] = describe(len(made), src, dst, dev)
        made[key].start()

    def arrived(key):
        made[key].wait_recv()

    own_b = pltpu.make_async_copy(b_ref, bbuf.at[core], lsem.at[0])
    own_l = pltpu.make_async_copy(l_ref, lbuf.at[core], lsem.at[1])
    own_b.start()
    own_l.start()

    for at_col in range(0, half_k, 1024):
        left = a_ref[:, at_col : at_col + 1024].astype(F32)
        right = a_ref[:, half_k + at_col : half_k + at_col + 1024].astype(F32)
        abuf[0, p, :, at_col : at_col + 1024] = left[:16].astype(BF16)
        abuf[0, p, :, half_k + at_col : half_k + at_col + 1024] = right[:16].astype(BF16)
        abuf[0, p, :, width + at_col : width + at_col + 1024] = jnp.concatenate([left[16:], right[16:]], axis=0).astype(BF16)

    pl.semaphore_wait(barrier, len(partners))

    halves = (pl.ds(0, relay), pl.ds(relay, relay))

    def along_first(way, h):
        send(("a1", way, h), abuf.at[0, p, :, halves[h]], abuf.at[0, p, :, halves[h]], at(p + way, q))

    def spread(i):
        pp = (p + i) % RING
        for n in range(2):
            send(("a2", i, 1, n), abuf.at[0, pp, :, halves[n]], abuf.at[3, pp, :, halves[n]], at(p, q + 1))
            m = 1 - n
            send(("a2", i, -1, m), abuf.at[0, pp, :, halves[m]], abuf.at[1, pp, :, halves[m]], at(p, q - 1))

    def pass_on(i):
        pp = (p + i) % RING
        arrived(("a2", i, 1, 0))
        send(("a2r", i, 1), abuf.at[3, pp, :, halves[0]], abuf.at[2, pp, :, halves[0]], at(p, q + 1))
        arrived(("a2", i, -1, 1))
        send(("a2r", i, -1), abuf.at[1, pp, :, halves[1]], abuf.at[2, pp, :, halves[1]], at(p, q - 1))

    along_first(1, 0)
    along_first(-1, 1)
    along_first(1, 1)
    along_first(-1, 0)
    to_sister = on_chip(z, sister)
    send("b", b_ref, bbuf.at[core], to_sister)
    send("l", l_ref, lbuf.at[core], to_sister)

    def amps_of(cc, keep):
        for fq in range(RING):
            for pair in range(0, RING, 2):
                tails = []
                for fp in (pair, pair + 1):
                    chip = fp * 4 + fq if cc == 0 else fq * 4 + fp
                    block = amp_ref[48 * chip : 48 * chip + 48, :].astype(F32)
                    block = block[24 * cc : 24 * cc + 24]
                    keep[fq, 16 * fp : 16 * fp + 16, :] = block[:16].astype(BF16)
                    tails.append(block[16:])
                keep[fq, 64 + 8 * pair : 80 + 8 * pair, :] = jnp.concatenate(tails, axis=0).astype(BF16)

    @pl.when(core == 0)
    def _():
        amps_of(0, amps_mine)
        amps_of(1, amps_away)

    @pl.when(core == 1)
    def _():
        amps_of(1, amps_mine)
        amps_of(0, amps_away)

    send("amp", amps_away, ampbuf, to_sister)

    pp, pm = (p + 1) % RING, (p + 3) % RING
    arrived(("a1", 1, 0))
    send(("a1r", 1), abuf.at[0, pm, :, halves[0]], abuf.at[0, pm, :, halves[0]], at(p + 1, q))
    arrived(("a1", -1, 1))
    send(("a1r", -1), abuf.at[0, pp, :, halves[1]], abuf.at[0, pp, :, halves[1]], at(p - 1, q))
    spread(0)
    for part in range(eo_ref.shape[0] // 128):
        values = jnp.broadcast_to(eo_ref[part * 128 : part * 128 + 128].reshape(1, 128), (128, 128))
        occ[part * 128 : part * 128 + 128, :] = values.T
    arrived(("a1", 1, 1))
    spread(3)
    arrived(("a1", -1, 0))
    spread(1)
    arrived(("a1r", 1))
    arrived(("a1r", -1))
    spread(2)

    def multiply(j, then=lambda n: None):
        row = (q + j) % RING

        def one_tile(n, carry):
            cc = (core + n // 2) % 2
            t = cc * 2 + n % 2
            cols = pl.ds(pl.multiple_of((t % 2) * 256, 256), 256)

            def one_part(n, sums):
                start = pl.multiple_of(n * PART, PART)

                def block(first):
                    return abuf[j, :, :, pl.ds(first + start, PART)].reshape(64, PART)

                def product(first):
                    return jnp.dot(
                        jnp.concatenate([block(first), block(width)], axis=0), bbuf[cc, pl.ds(first + start, PART), cols],
                        preferred_element_type=F32,
                    )

                return sums[0] + product(0), sums[1] + product(half_k)

            zero = jnp.zeros((128, 256), F32)
            sum0, sum1 = lax.fori_loop(0, half_k // PART, one_part, (zero, zero))
            main_rows = sum0[:64] + sum1[:64]
            tail_rows = sum0[64:].reshape(4, 2, 8, 256)[:, 0] + sum1[64:].reshape(4, 2, 8, 256)[:, 1]
            cycle = jnp.concatenate([main_rows, tail_rows.reshape(32, 256)], axis=0).astype(BF16)
            cyc[j, t] = cycle
            amps = jnp.where(cc == core, amps_mine[row, :, cols].astype(F32), ampbuf[row, :, cols].astype(F32))
            rows[j][p * 4 + t] = (amps + cycle.astype(F32)).astype(BF16)
            return carry

        def two_tiles(n, carry):
            lax.fori_loop(2 * n, 2 * n + 2, one_tile, 0)
            then(n)
            return carry

        lax.fori_loop(0, 2, two_tiles, 0)

    def share(j):
        base = len(made)

        def both_ways(n):
            two = pl.ds(p * 4 + 2 * ((core + n) % 2), 2)
            return [describe(base + 2 * n + w, rows[j].at[two], rows[j].at[two], at(p + way, q)) for w, way in enumerate((1, -1))]

        for n in range(2):
            made["e1", j, 1, n], made["e1", j, -1, n] = both_ways(n)

        def start(n):
            for one in both_ways(n):
                one.start()

        return start

    def share_on(j):
        for n, way, source in ((0, 1, pm), (1, -1, pp)):
            arrived(("e1", j, way, n))
            two = pl.ds(source * 4 + 2 * ((core + n) % 2), 2)
            send(("e1r", j, n), rows[j].at[two], rows[j].at[two], at(p + way, q))

    def hand_out(j):
        arrived(("e1", j, 1, 1))
        arrived(("e1", j, -1, 0))
        arrived(("e1r", j, 0))
        arrived(("e1r", j, 1))
        for g in (2, 0, 1):
            d = DIST[g]

            def one_slot(s, carry, g=g):
                packs[j, bases[g] + s] = rows[j][plan[g, s]]
                return carry

            lax.fori_loop(0, sizes[g], one_slot, 0)
            there = DIST.index((-d) % RING)
            send(
                ("e2", j, g), packs.at[j, pl.ds(bases[g], sizes[g])],
                got[(j - d) % RING].at[pl.ds(bases[there], sizes[there])], at(p, q + d),
            )

    pass_on(0)
    own_b.wait()
    arrived("amp")
    pass_on(3)
    arrived("b")
    multiply(0)
    pass_on(1)
    own_l.wait()
    arrived("l")
    mine = (x * 4 + y) * 4

    def mask_weights(s, carry):
        t, k = s // 4, s % 4
        slot = (t % 2) * 4 + k
        lbuf[t // 2, slot] = lbuf[t // 2, slot] * plan[16 + k, mine + t].astype(F32).astype(BF16)
        return carry

    lax.fori_loop(0, 16, mask_weights, 0)
    pass_on(2)
    start = share(0)
    start(0)
    start(1)
    for i in range(RING):
        arrived(("a2", i, 1, 1))
    multiply(3, share(3))
    share_on(0)
    for i in range(RING):
        arrived(("a2", i, -1, 0))
    multiply(1, share(1))
    share_on(3)
    share_on(1)
    for i in range(RING):
        arrived(("a2r", i, 1))
        arrived(("a2r", i, -1))
    hand_out(0)
    multiply(2, share(2))
    hand_out(3)
    hand_out(1)
    share_on(2)
    hand_out(2)

    nacc[...] = jnp.zeros_like(nacc)

    def finish(*chunks):
        for j in chunks:
            for g, d in enumerate(DIST):
                arrived(("e2", (j - d) % RING, DIST.index((-d) % RING)))

        def one_tile(t, carry):
            cols = pl.ds(pl.multiple_of((t % 2) * 256, 256), 256)
            total = jnp.zeros((96 * len(chunks), 256), F32)
            for k in range(4):
                parts = []
                for j in chunks:
                    near = rows[j][plan[4 + k, mine + t]].astype(F32)
                    far = got[j][plan[8 + k, mine + t]].astype(F32)
                    parts.append(jnp.where(plan[12 + k, mine + t] == 1, near, far).astype(BF16))
                block = jnp.concatenate(parts, axis=0)
                total += jnp.dot(block, lbuf[t // 2, (t % 2) * 4 + k], preferred_element_type=F32)
            for n, j in enumerate(chunks):
                residual = (total[96 * n : 96 * n + 96] + cyc[j, t].astype(F32)).astype(BF16)
                wide = residual.astype(F32)
                resbuf[t // 2, (q + j) % RING, :, cols] = residual
                nacc[...] += (wide * wide).reshape(12, 8, 256).sum(axis=0)
            return carry

        lax.fori_loop(0, 4, one_tile, 0)
        for j in chunks:
            row = (q + j) % RING
            send(("res", j), resbuf.at[sister, row], resin.at[row], to_sister)

    finish(2)
    finish(0, 3, 1)

    def write(first, last):
        def rows_of(cc, fq, fp):
            pair = 64 + 16 * (fp // 2)
            head = jnp.where(core == cc, resbuf[cc, fq, 16 * fp : 16 * fp + 16, :].astype(F32), resin[fq, 16 * fp : 16 * fp + 16, :].astype(F32))
            tail = jnp.where(core == cc, resbuf[cc, fq, pair : pair + 16, :].astype(F32), resin[fq, pair : pair + 16, :].astype(F32))
            return [head, tail[8 * (fp % 2) : 8 * (fp % 2) + 8]]

        for chip in range(first, last):
            fx, fy = chip // 4, chip % 4
            block = jnp.concatenate(rows_of(0, fy, fx) + rows_of(1, fx, fy), axis=0)
            here = slice(48 * chip, 48 * chip + 48)
            lanes = occ[here, :]
            denom = jnp.concatenate([lanes] * (block.shape[1] // 128), axis=1) + ev_ref[...]
            res_ref[here, :] = block.astype(BF16)
            new_ref[here, :] = (amp_ref[here, :].astype(F32) - block / denom).astype(BF16)

    def spread_norm(stage, slot, value, devices):
        nbuf[stage, slot] = value
        for n, dev in enumerate(devices):
            send(("n", stage, n), nbuf.at[stage, slot], nbuf.at[stage, slot], dev)

    def sum_norm(stage, devices):
        for n in range(len(devices)):
            arrived(("n", stage, n))
        total = nbuf[stage, 0]
        for n in range(1, len(devices) + 1):
            total = total + nbuf[stage, n]
        return total

    earlier = list(made.values())
    spread_norm(0, z * 2 + core, nacc[:, 0:128] + nacc[:, 128:256], group)
    for j in range(RING):
        arrived(("res", j))
    write(0, 8)
    for one in earlier:
        one.wait_send()
    spread_norm(1, p * 4 + q, sum_norm(0, group), plane)
    write(8, 16)
    norm_ref[0] = jnp.sum(sum_norm(1, plane))
    for one in list(made.values())[len(earlier) :]:
        one.wait_send()


COPIES = 96


def run_main(caps, number, plan, a, b, amp, blocks, eo, ev):
    width, columns = b.shape
    rows = amp.shape[0] // 8
    smem, vmem = pl.BlockSpec(memory_space=pltpu.SMEM), pl.BlockSpec(memory_space=pltpu.VMEM)
    anywhere = pl.BlockSpec(memory_space=pl.ANY)
    out = jax.ShapeDtypeStruct(amp.shape, BF16)
    row_buf = pltpu.VMEM((16, rows, 256), BF16)
    got_buf = pltpu.VMEM((2 * caps[0] + caps[1], rows, 256), BF16)
    part = pltpu.VMEM((RING, rows, columns), BF16)
    return pl.pallas_call(
        functools.partial(main, caps, width),
        out_shape=(out, out, jax.ShapeDtypeStruct((1,), F32)),
        in_specs=[smem, vmem, anywhere, vmem, anywhere, vmem, vmem],
        out_specs=(vmem, vmem, smem),
        scratch_shapes=[
            pltpu.VMEM((RING, RING, 16, width + width // 2), BF16),
            pltpu.VMEM((2, width, columns), BF16),
            part, part, part,
            pltpu.VMEM((2, 8, 256, 256), BF16),
            pltpu.VMEM((amp.shape[0], 128), F32),
            pltpu.VMEM((RING, 4, rows, 256), BF16),
            row_buf, row_buf, row_buf, row_buf,
            pltpu.VMEM((RING, 2 * caps[0] + caps[1], rows, 256), BF16),
            got_buf, got_buf, got_buf, got_buf,
            pltpu.VMEM((2, RING, rows, columns), BF16),
            part,
            pltpu.VMEM((8, 256), F32),
            pltpu.VMEM((2, 16, 8, 128), F32),
            pltpu.SemaphoreType.DMA((COPIES,)),
            pltpu.SemaphoreType.DMA((COPIES,)),
            pltpu.SemaphoreType.DMA((2,)),
        ],
        compiler_params=pltpu.CompilerParams(
            collective_id=number, has_side_effects=True, vmem_limit_bytes=60 * 2**20
        ),
        cost_estimate=pl.CostEstimate(flops=8 * 10**9, bytes_accessed=20 * 2**20, transcendentals=0),
    )(plan, a, b, amp, blocks, eo, ev)


def on_device(amps, cycle_amps, cycle_ints, ladder_ints, sources, counts, eps_occ, eps_vir):
    plan, which = make_tables(sources, counts)
    blocks = ladder_ints.reshape(8, *ladder_ints.shape[2:])
    branches = [functools.partial(run_main, caps, n) for n, caps in enumerate(CAPS)]
    residual, new_amps, norm = lax.switch(
        which[0], branches, plan, cycle_amps, cycle_ints, amps, blocks, eps_occ, eps_vir.reshape(1, -1)
    )
    return residual, new_amps, norm[0]


def solution(mesh):
    placed = (
        P("occ", "vir"),
        P(("occ", "vir"), None),
        P(None, "vir"),
        P("vir", None, None, None),
        P(),
        P(),
        P("occ"),
        P("vir"),
    )
    return jax.shard_map(
        on_device,
        mesh=mesh,
        in_specs=placed,
        out_specs=(P("occ", "vir"), P("occ", "vir"), P()),
        check_vma=False,
    )
```

```python
import functools

import jax
import jax.numpy as jnp
from jax import lax
from jax.experimental import pallas as pl
from jax.experimental.pallas import tpu as pltpu
from jax.sharding import PartitionSpec as P

MESH = pl.DeviceIdType.MESH
RING = 4
DIST = (1, 3, 2)
CAPS = ((5, 5), (6, 5), (5, 6), (6, 6), (7, 7), (8, 8), (16, 16))
PART = 2048
F32, BF16 = jnp.float32, jnp.bfloat16


def place():
    vir = lax.axis_index("vir")
    core = vir % 2
    y = (vir // 2) % RING
    x = vir // (2 * RING)
    first = jnp.where(core == 0, x, y)
    second = jnp.where(core == 0, y, x)
    return core, first, second, x, y


def tables(sources, counts, plan, which):
    core, p, q, x, y = place()

    def iota(shape, axis):
        return lax.broadcasted_iota(jnp.int32, shape, axis)

    def ones(mask):
        return jnp.where(mask, 1.0, 0.0)

    def dot(one, other):
        return jnp.dot(one.astype(BF16), other.astype(BF16), preferred_element_type=F32)

    def split(tile):
        tx, ty = tile // 16, (tile // 4) % 4
        return jnp.where(core == 0, tx, ty), jnp.where(core == 0, ty, tx), tile % 4

    tile = iota((64, 64), 0)
    hits = jnp.zeros((64, 64), F32)
    for k in range(4):
        hits += ones((sources[k : k + 1, :] == tile) & (counts[...] > k))
    need = jnp.minimum(dot(hits, ones(iota((64, 128), 0) // 4 == iota((64, 128), 1))), 1.0)

    line, member = iota((16, 64), 0), iota((16, 64), 1)
    inside = ((line < 4) & ((member // 4) % 4 == line)) | ((line >= 4) & (line < 8) & (member // 16 == line - 4))
    line, chip = iota((16, 128), 0), iota((16, 128), 1)
    sums = dot(ones(inside), need)
    away = jnp.where(line < 4, line - chip % 4, line - 4 - chip // 4)
    next_line = (away == 1) | (away == -1) | (away == 3) | (away == -3)
    far_line = (away == 2) | (away == -2)
    most = jnp.max(jnp.where(next_line, sums, 0.0)).astype(jnp.int32)
    most_far = jnp.max(jnp.where(far_line, sums, 0.0)).astype(jnp.int32)
    branch, cap = jnp.int32(len(CAPS) - 1), jnp.int32(CAPS[-1][0])
    for n in range(len(CAPS) - 2, -1, -1):
        enough = (most <= CAPS[n][0]) & (most_far <= CAPS[n][1])
        branch = jnp.where(enough, n, branch)
        cap = jnp.where(enough, CAPS[n][0], cap)
    which[0] = branch

    tp, tq, tt = split(tile)
    op, oq, ot = split(iota((64, 64), 1))
    placed = dot(ones((tq == oq) & (op * 4 + ot < tp * 4 + tt)), need)
    sp, sq, st = split(iota((64, 1), 0))
    entry = (sp * 4 + st).astype(F32)
    chip, slot = iota((64, 128), 1), iota((64, 128), 1).astype(F32)
    plan[...] = jnp.zeros_like(plan)
    for g, d in enumerate(DIST):
        other = (q + d) % RING
        there = chip == jnp.where(core == 0, p * 4 + other, other * 4 + p)
        wants = jnp.sum(jnp.where(there, need, 0.0), axis=1, keepdims=True)
        where = jnp.sum(jnp.where(there, placed, 0.0), axis=1, keepdims=True)
        taken = (wants > 0.0) & (sq == q) & (where == slot)
        plan[g : g + 1, :] = jnp.sum(jnp.where(taken, entry, 0.0), axis=0, keepdims=True).astype(jnp.int32)
    where = jnp.sum(jnp.where(chip == x * 4 + y, placed, 0.0), axis=1, keepdims=True)
    for k in range(4):
        source = sources[k : k + 1, :]
        tp, tq, tt = split(source)
        after = jnp.sum(jnp.where(source == tile, where, 0.0), axis=0, keepdims=True).astype(jnp.int32)
        live = counts[...] > k
        near = tq == q
        d = (tq - q + RING) % RING
        group = jnp.where(d == 1, 0, jnp.where(d == 3, 1, 2))
        plan[4 + k : 5 + k, 0:64] = jnp.where(live & near, tp * 4 + tt, p * 4)
        plan[8 + k : 9 + k, 0:64] = jnp.where(live & ~near, group * cap + after, 0)
        plan[12 + k : 13 + k, 0:64] = jnp.where(live & ~near, 0, 1)
        plan[16 + k : 17 + k, 0:64] = jnp.where(live, 1, 0)


def make_tables(sources, counts):
    smem, vmem = pl.BlockSpec(memory_space=pltpu.SMEM), pl.BlockSpec(memory_space=pltpu.VMEM)
    return pl.pallas_call(
        tables,
        out_shape=(jax.ShapeDtypeStruct((24, 128), jnp.int32), jax.ShapeDtypeStruct((1,), jnp.int32)),
        in_specs=[vmem, vmem],
        out_specs=(vmem, smem),
    )(sources.T, counts.reshape(1, -1))


def main(
    caps, width, plan, a_ref, b_ref, amp_ref, l_ref, eo_ref, ev_ref,
    res_ref, new_ref, norm_ref,
    abuf, bbuf, amps_mine, amps_away, ampbuf, lbuf, occ, cyc, row0, row1, row2, row3, packs, got0, got1, got2, got3,
    resbuf, resin, nacc, nbuf, ssem, rsem, lsem,
):
    core, p, q, x, y = place()
    z = lax.axis_index("occ")
    sister = 1 - core
    rows, got = (row0, row1, row2, row3), (got0, got1, got2, got3)
    half_k = width // 2
    relay = 3 * half_k // 2
    sizes = (caps[0], caps[0], caps[1])
    bases = (0, caps[0], 2 * caps[0])

    def at(fp, fq):
        fp, fq = fp % RING, fq % RING
        return (z, jnp.where(core == 0, (fp * 4 + fq) * 2, (fq * 4 + fp) * 2 + 1))

    def on_chip(zz, cc):
        return (zz, (x * 4 + y) * 2 + cc)

    group = [on_chip((z + dz) % 4, (core + dc) % 2) for dz in (2, 1, 3, 0) for dc in (1, 0) if dz or dc]
    plane = [at(p + dp, q + dq) for dp in (2, 1, 3, 0) for dq in (2, 1, 3, 0) if dp or dq]
    partners = group + plane
    barrier = pltpu.get_barrier_semaphore()
    for one in partners:
        pl.semaphore_signal(barrier, inc=1, device_id=one, device_id_type=MESH)

    made = {}

    def describe(n, src, dst, dev):
        return pltpu.make_async_remote_copy(
            src_ref=src, dst_ref=dst, send_sem=ssem.at[n], recv_sem=rsem.at[n], device_id=dev, device_id_type=MESH
        )

    def send(key, src, dst, dev):
        made[key] = describe(len(made), src, dst, dev)
        made[key].start()

    def arrived(key):
        made[key].wait_recv()

    own_b = pltpu.make_async_copy(b_ref, bbuf.at[core], lsem.at[0])
    own_l = pltpu.make_async_copy(l_ref, lbuf.at[core], lsem.at[1])
    own_b.start()
    own_l.start()

    for at_col in range(0, half_k, 1024):
        left = a_ref[:, at_col : at_col + 1024].astype(F32)
        right = a_ref[:, half_k + at_col : half_k + at_col + 1024].astype(F32)
        abuf[0, p, :, at_col : at_col + 1024] = left[:16].astype(BF16)
        abuf[0, p, :, half_k + at_col : half_k + at_col + 1024] = right[:16].astype(BF16)
        abuf[0, p, :, width + at_col : width + at_col + 1024] = jnp.concatenate([left[16:], right[16:]], axis=0).astype(BF16)

    pl.semaphore_wait(barrier, len(partners))

    halves = (pl.ds(0, relay), pl.ds(relay, relay))

    def along_first(way, h):
        send(("a1", way, h), abuf.at[0, p, :, halves[h]], abuf.at[0, p, :, halves[h]], at(p + way, q))

    def spread(i):
        pp = (p + i) % RING
        for n in range(2):
            send(("a2", i, 1, n), abuf.at[0, pp, :, halves[n]], abuf.at[3, pp, :, halves[n]], at(p, q + 1))
            m = 1 - n
            send(("a2", i, -1, m), abuf.at[0, pp, :, halves[m]], abuf.at[1, pp, :, halves[m]], at(p, q - 1))

    def pass_on(i):
        pp = (p + i) % RING
        arrived(("a2", i, 1, 0))
        send(("a2r", i, 1), abuf.at[3, pp, :, halves[0]], abuf.at[2, pp, :, halves[0]], at(p, q + 1))
        arrived(("a2", i, -1, 1))
        send(("a2r", i, -1), abuf.at[1, pp, :, halves[1]], abuf.at[2, pp, :, halves[1]], at(p, q - 1))

    along_first(1, 0)
    along_first(-1, 1)
    along_first(1, 1)
    along_first(-1, 0)
    to_sister = on_chip(z, sister)
    send("b", b_ref, bbuf.at[core], to_sister)
    send("l", l_ref, lbuf.at[core], to_sister)

    def amps_of(cc, keep):
        for fq in range(RING):
            for pair in range(0, RING, 2):
                tails = []
                for fp in (pair, pair + 1):
                    chip = fp * 4 + fq if cc == 0 else fq * 4 + fp
                    block = amp_ref[48 * chip : 48 * chip + 48, :].astype(F32)
                    block = block[24 * cc : 24 * cc + 24]
                    keep[fq, 16 * fp : 16 * fp + 16, :] = block[:16].astype(BF16)
                    tails.append(block[16:])
                keep[fq, 64 + 8 * pair : 80 + 8 * pair, :] = jnp.concatenate(tails, axis=0).astype(BF16)

    @pl.when(core == 0)
    def _():
        amps_of(0, amps_mine)
        amps_of(1, amps_away)

    @pl.when(core == 1)
    def _():
        amps_of(1, amps_mine)
        amps_of(0, amps_away)

    send("amp", amps_away, ampbuf, to_sister)

    pp, pm = (p + 1) % RING, (p + 3) % RING
    arrived(("a1", 1, 0))
    send(("a1r", 1), abuf.at[0, pm, :, halves[0]], abuf.at[0, pm, :, halves[0]], at(p + 1, q))
    arrived(("a1", -1, 1))
    send(("a1r", -1), abuf.at[0, pp, :, halves[1]], abuf.at[0, pp, :, halves[1]], at(p - 1, q))
    spread(0)
    for part in range(eo_ref.shape[0] // 128):
        values = jnp.broadcast_to(eo_ref[part * 128 : part * 128 + 128].reshape(1, 128), (128, 128))
        occ[part * 128 : part * 128 + 128, :] = values.T
    arrived(("a1", 1, 1))
    spread(3)
    arrived(("a1", -1, 0))
    spread(1)
    arrived(("a1r", 1))
    arrived(("a1r", -1))
    spread(2)

    def multiply(j, then=lambda n: None):
        row = (q + j) % RING

        def one_tile(n, carry):
            cc = (core + n // 2) % 2
            t = cc * 2 + n % 2
            cols = pl.ds(pl.multiple_of((t % 2) * 256, 256), 256)

            def one_part(n, sums):
                start = pl.multiple_of(n * PART, PART)

                def block(first):
                    return abuf[j, :, :, pl.ds(first + start, PART)].reshape(64, PART)

                def product(first):
                    return jnp.dot(
                        jnp.concatenate([block(first), block(width)], axis=0), bbuf[cc, pl.ds(first + start, PART), cols],
                        preferred_element_type=F32,
                    )

                return sums[0] + product(0), sums[1] + product(half_k)

            zero = jnp.zeros((128, 256), F32)
            sum0, sum1 = lax.fori_loop(0, half_k // PART, one_part, (zero, zero))
            main_rows = sum0[:64] + sum1[:64]
            tail_rows = sum0[64:].reshape(4, 2, 8, 256)[:, 0] + sum1[64:].reshape(4, 2, 8, 256)[:, 1]
            cycle = jnp.concatenate([main_rows, tail_rows.reshape(32, 256)], axis=0).astype(BF16)
            cyc[j, t] = cycle
            amps = jnp.where(cc == core, amps_mine[row, :, cols].astype(F32), ampbuf[row, :, cols].astype(F32))
            rows[j][p * 4 + t] = (amps + cycle.astype(F32)).astype(BF16)
            return carry

        def two_tiles(n, carry):
            lax.fori_loop(2 * n, 2 * n + 2, one_tile, 0)
            then(n)
            return carry

        lax.fori_loop(0, 2, two_tiles, 0)

    def share(j):
        base = len(made)

        def both_ways(n):
            two = pl.ds(p * 4 + 2 * ((core + n) % 2), 2)
            return [describe(base + 2 * n + w, rows[j].at[two], rows[j].at[two], at(p + way, q)) for w, way in enumerate((1, -1))]

        for n in range(2):
            made["e1", j, 1, n], made["e1", j, -1, n] = both_ways(n)

        def start(n):
            for one in both_ways(n):
                one.start()

        return start

    def share_on(j):
        for n, way, source in ((0, 1, pm), (1, -1, pp)):
            arrived(("e1", j, way, n))
            two = pl.ds(source * 4 + 2 * ((core + n) % 2), 2)
            send(("e1r", j, n), rows[j].at[two], rows[j].at[two], at(p + way, q))

    def hand_out(j):
        arrived(("e1", j, 1, 1))
        arrived(("e1", j, -1, 0))
        arrived(("e1r", j, 0))
        arrived(("e1r", j, 1))
        for g in (2, 0, 1):
            d = DIST[g]

            def one_slot(s, carry, g=g):
                packs[j, bases[g] + s] = rows[j][plan[g, s]]
                return carry

            lax.fori_loop(0, sizes[g], one_slot, 0)
            there = DIST.index((-d) % RING)
            send(
                ("e2", j, g), packs.at[j, pl.ds(bases[g], sizes[g])],
                got[(j - d) % RING].at[pl.ds(bases[there], sizes[there])], at(p, q + d),
            )

    pass_on(0)
    own_b.wait()
    arrived("amp")
    pass_on(3)
    arrived("b")
    multiply(0)
    pass_on(1)
    own_l.wait()
    arrived("l")
    mine = (x * 4 + y) * 4

    def mask_weights(s, carry):
        t, k = s // 4, s % 4
        slot = (t % 2) * 4 + k
        lbuf[t // 2, slot] = lbuf[t // 2, slot] * plan[16 + k, mine + t].astype(F32).astype(BF16)
        return carry

    lax.fori_loop(0, 16, mask_weights, 0)
    pass_on(2)
    start = share(0)
    start(0)
    start(1)
    for i in range(RING):
        arrived(("a2", i, 1, 1))
    multiply(3, share(3))
    share_on(0)
    for i in range(RING):
        arrived(("a2", i, -1, 0))
    multiply(1, share(1))
    share_on(3)
    share_on(1)
    for i in range(RING):
        arrived(("a2r", i, 1))
        arrived(("a2r", i, -1))
    hand_out(0)
    multiply(2, share(2))
    hand_out(3)
    hand_out(1)
    share_on(2)
    hand_out(2)

    nacc[...] = jnp.zeros_like(nacc)

    def finish(*chunks):
        for j in chunks:
            for g, d in enumerate(DIST):
                arrived(("e2", (j - d) % RING, DIST.index((-d) % RING)))

        def one_tile(t, carry):
            cols = pl.ds(pl.multiple_of((t % 2) * 256, 256), 256)
            total = jnp.zeros((96 * len(chunks), 256), F32)
            for k in range(4):
                parts = []
                for j in chunks:
                    near = rows[j][plan[4 + k, mine + t]].astype(F32)
                    far = got[j][plan[8 + k, mine + t]].astype(F32)
                    parts.append(jnp.where(plan[12 + k, mine + t] == 1, near, far).astype(BF16))
                block = jnp.concatenate(parts, axis=0)
                total += jnp.dot(block, lbuf[t // 2, (t % 2) * 4 + k], preferred_element_type=F32)
            for n, j in enumerate(chunks):
                residual = (total[96 * n : 96 * n + 96] + cyc[j, t].astype(F32)).astype(BF16)
                wide = residual.astype(F32)
                resbuf[t // 2, (q + j) % RING, :, cols] = residual
                nacc[...] += (wide * wide).reshape(12, 8, 256).sum(axis=0)
            return carry

        lax.fori_loop(0, 4, one_tile, 0)
        for j in chunks:
            row = (q + j) % RING
            send(("res", j), resbuf.at[sister, row], resin.at[row], to_sister)

    finish(2)
    finish(0, 3, 1)

    def write(first, last):
        def rows_of(cc, fq, fp):
            pair = 64 + 16 * (fp // 2)
            head = jnp.where(core == cc, resbuf[cc, fq, 16 * fp : 16 * fp + 16, :].astype(F32), resin[fq, 16 * fp : 16 * fp + 16, :].astype(F32))
            tail = jnp.where(core == cc, resbuf[cc, fq, pair : pair + 16, :].astype(F32), resin[fq, pair : pair + 16, :].astype(F32))
            return [head, tail[8 * (fp % 2) : 8 * (fp % 2) + 8]]

        for chip in range(first, last):
            fx, fy = chip // 4, chip % 4
            block = jnp.concatenate(rows_of(0, fy, fx) + rows_of(1, fx, fy), axis=0)
            here = slice(48 * chip, 48 * chip + 48)
            lanes = occ[here, :]
            denom = jnp.concatenate([lanes] * (block.shape[1] // 128), axis=1) + ev_ref[...]
            res_ref[here, :] = block.astype(BF16)
            new_ref[here, :] = (amp_ref[here, :].astype(F32) - block / denom).astype(BF16)

    def spread_norm(stage, slot, value, devices):
        nbuf[stage, slot] = value
        for n, dev in enumerate(devices):
            send(("n", stage, n), nbuf.at[stage, slot], nbuf.at[stage, slot], dev)

    def sum_norm(stage, devices):
        for n in range(len(devices)):
            arrived(("n", stage, n))
        total = nbuf[stage, 0]
        for n in range(1, len(devices) + 1):
            total = total + nbuf[stage, n]
        return total

    earlier = list(made.values())
    spread_norm(0, z * 2 + core, nacc[:, 0:128] + nacc[:, 128:256], group)
    for j in range(RING):
        arrived(("res", j))
    write(0, 8)
    for one in earlier:
        one.wait_send()
    spread_norm(1, p * 4 + q, sum_norm(0, group), plane)
    write(8, 16)
    norm_ref[0] = jnp.sum(sum_norm(1, plane))
    for one in list(made.values())[len(earlier) :]:
        one.wait_send()


COPIES = 96


def run_main(caps, number, plan, a, b, amp, blocks, eo, ev):
    width, columns = b.shape
    rows = amp.shape[0] // 8
    smem, vmem = pl.BlockSpec(memory_space=pltpu.SMEM), pl.BlockSpec(memory_space=pltpu.VMEM)
    anywhere = pl.BlockSpec(memory_space=pl.ANY)
    out = jax.ShapeDtypeStruct(amp.shape, BF16)
    row_buf = pltpu.VMEM((16, rows, 256), BF16)
    got_buf = pltpu.VMEM((2 * caps[0] + caps[1], rows, 256), BF16)
    part = pltpu.VMEM((RING, rows, columns), BF16)
    return pl.pallas_call(
        functools.partial(main, caps, width),
        out_shape=(out, out, jax.ShapeDtypeStruct((1,), F32)),
        in_specs=[smem, vmem, anywhere, vmem, anywhere, vmem, vmem],
        out_specs=(vmem, vmem, smem),
        scratch_shapes=[
            pltpu.VMEM((RING, RING, 16, width + width // 2), BF16),
            pltpu.VMEM((2, width, columns), BF16),
            part, part, part,
            pltpu.VMEM((2, 8, 256, 256), BF16),
            pltpu.VMEM((amp.shape[0], 128), F32),
            pltpu.VMEM((RING, 4, rows, 256), BF16),
            row_buf, row_buf, row_buf, row_buf,
            pltpu.VMEM((RING, 2 * caps[0] + caps[1], rows, 256), BF16),
            got_buf, got_buf, got_buf, got_buf,
            pltpu.VMEM((2, RING, rows, columns), BF16),
            part,
            pltpu.VMEM((8, 256), F32),
            pltpu.VMEM((2, 16, 8, 128), F32),
            pltpu.SemaphoreType.DMA((COPIES,)),
            pltpu.SemaphoreType.DMA((COPIES,)),
            pltpu.SemaphoreType.DMA((2,)),
        ],
        compiler_params=pltpu.CompilerParams(
            collective_id=number, has_side_effects=True, vmem_limit_bytes=60 * 2**20
        ),
        cost_estimate=pl.CostEstimate(flops=8 * 10**9, bytes_accessed=20 * 2**20, transcendentals=0),
    )(plan, a, b, amp, blocks, eo, ev)


def on_device(amps, cycle_amps, cycle_ints, ladder_ints, sources, counts, eps_occ, eps_vir):
    plan, which = make_tables(sources, counts)
    blocks = ladder_ints.reshape(8, *ladder_ints.shape[2:])
    branches = [functools.partial(run_main, caps, n) for n, caps in enumerate(CAPS)]
    residual, new_amps, norm = lax.switch(
        which[0], branches, plan, cycle_amps, cycle_ints, amps, blocks, eps_occ, eps_vir.reshape(1, -1)
    )
    return residual, new_amps, norm[0]


def solution(mesh):
    placed = (
        P("occ", "vir"),
        P(("occ", "vir"), None),
        P(None, "vir"),
        P("vir", None, None, None),
        P(),
        P(),
        P("occ"),
        P("vir"),
    )
    return jax.shard_map(
        on_device,
        mesh=mesh,
        in_specs=placed,
        out_specs=(P("occ", "vir"), P("occ", "vir"), P()),
        check_vma=False,
    )
```
